256 devices in a mesh: tm: 8 (over z_hi, y), node: 32 (over x, z_lo, core).
Axes of the slice: x: 4, y: 4, z: 8 (z_hi: 2, z_lo: 4; z = z_hi * 4 + z_lo), core: 2. Of those that a mesh axis runs over, the one named last changes fastest.
Arguments:
- thermal_loading: bfloat16 [64, 4096], P(None, 'tm'), may hold values from -12 to 12
- forcing_matrix: bfloat16 [2048, 64], P('node'), may hold values from -0.75 to 0.75
- lagged_responses: float32 [2048, 256], P('node'), may hold values from 0 to 3, as said below
- pattern_heat_matrix: bfloat16 [2048, 32768], P(None, 'node'), may hold values from -0.03125 to 0.03125
- pattern_loading_matrix: bfloat16 [2048, 32768], P(None, 'node'), may hold values from -0.09375 to 0.09375
- starting_scale_depth: float32 [32768], P('node'), may hold values from 0.05 to 0.3
- point_parabolic_speed: float32 [32768], P('node'), may hold values from 1 to 3
Outputs:
- bond_heat_excursion: float32 [4096, 32768], P('tm', 'node')
- bond_loading: float32 [4096, 32768], P('tm', 'node')
- grown_layer_depth: float32 [4096, 32768], P('tm', 'node')
- fatigue_harm: float32 [4096, 32768], P('tm', 'node')
The draws below stay inside these ranges and needn't reach their ends.
Inputs may be any that keep to these rules, and one draw needn't show every extreme that they name: `lagged_responses`: positive impulse responses.
All inputs are finite; a program needn't handle non-finite values.
Results may differ from the reference program's by a relative error of at most 0.0041.
Values may be sent and summed in bfloat16 or wider, within the bound.
A program may use at most 128 MiB of HBM per device.

```python
import math
import jax
import jax.numpy as jnp
from jax import lax

HEAT_PATTERNS = 2048
CHAN = 64
KERNEL = 256
TIME = 4096
FACE_POINTS = 32768


def draw_thermal_loading(key, part):
    key = jax.random.fold_in(key, 11)
    step_index = jnp.arange(TIME, dtype=jnp.int32)[None, :]
    envelope = jnp.where(step_index < max(KERNEL // 8, 1), 6.0, 1.0).astype(jnp.float32)
    noise_draw = jax.random.normal(key, (CHAN, TIME), jnp.float32)
    return jnp.clip(envelope * noise_draw, -12.0, 12.0).astype(jnp.bfloat16)


def draw_lagged_responses(key, part):
    key = jax.random.fold_in(key, 5)
    key_rate, key_rough, key_prompt = jax.random.split(key, 3)
    log_low, log_high = (math.log(0.1), math.log(8.0))
    decay_rate = jnp.exp(jax.random.uniform(key_rate, (HEAT_PATTERNS, 1), jnp.float32, log_low, log_high)) / KERNEL
    lag_steps = jnp.arange(KERNEL, dtype=jnp.float32)[None, :]
    rough_factor = jax.random.uniform(key_rough, (HEAT_PATTERNS, KERNEL), jnp.float32, 0.5, 1.5)
    scaling = jnp.sqrt((1.0 - jnp.exp(-2.0 * decay_rate)) / (1.0 - jnp.exp(-2.0 * decay_rate * KERNEL)))
    prompt_part = jax.random.uniform(key_prompt, (HEAT_PATTERNS, 1), jnp.float32, 1.0, 1.5)
    first_lag = (lag_steps == 0.0).astype(jnp.float32)
    return rough_factor * jnp.exp(-lag_steps * decay_rate) * scaling + prompt_part * first_lag


def block_levels(stream_key, extent, shards, low, high):
    def one(position, shards_of):
        steps = jax.random.uniform(jax.random.fold_in(jax.random.fold_in(stream_key, 6), position), (shards_of,), jnp.float32, low / len(shards), high / len(shards))
        return jnp.repeat(jnp.exp(steps), extent[position] // shards_of).reshape((-1,) + (1,) * (len(extent) - position - 1))

    factor_of = one(*shards[0])
    for cut in shards[1:]:
        factor_of = factor_of * one(*cut)
    return factor_of


def bell_draw(rng, extent, deviation, most, pieces=(), kind=jnp.bfloat16):
    entries = jax.random.normal(rng, extent, jnp.float32) * deviation
    if len(pieces) > 0:
        entries = block_levels(rng, extent, pieces, -0.22, 0.18) * entries
    return jnp.clip(entries, min=-most, max=most).astype(kind)


def setup_inputs(seed: int = 0) -> dict:
    arg_keys = jax.random.split(jax.random.key(seed), 8)
    thermal_loading = draw_thermal_loading(jax.random.fold_in(arg_keys[7], 71), 0)
    forcing_matrix = bell_draw(arg_keys[1], (HEAT_PATTERNS, CHAN), CHAN ** -0.5, 0.75, ((0, 32),))
    lagged_responses = draw_lagged_responses(jax.random.fold_in(arg_keys[7], 71), 0)
    pattern_heat_matrix = bell_draw(arg_keys[3], (HEAT_PATTERNS, FACE_POINTS), (16 * HEAT_PATTERNS) ** -0.5, 0.03125, ((1, 32),))
    pattern_loading_matrix = bell_draw(arg_keys[4], (HEAT_PATTERNS, FACE_POINTS), (2 * HEAT_PATTERNS) ** -0.5, 0.09375, ((1, 32),))
    starting_scale_depth = jnp.clip(0.05 + 0.25 * jax.random.uniform(arg_keys[5], (FACE_POINTS,), jnp.float32) ** block_levels(arg_keys[5], (FACE_POINTS,), ((0, 32),), -0.2, 0.2), 0.05, 0.3)
    point_parabolic_speed = jnp.clip(jnp.exp(math.log(3.0) - 1.0986123 * jax.random.uniform(arg_keys[6], (FACE_POINTS,), jnp.float32) ** block_levels(arg_keys[6], (FACE_POINTS,), ((0, 32),), -0.2, 0.2)), 1.0, 3.0)
    return dict(thermal_loading=thermal_loading, forcing_matrix=forcing_matrix, lagged_responses=lagged_responses, pattern_heat_matrix=pattern_heat_matrix, pattern_loading_matrix=pattern_loading_matrix, starting_scale_depth=starting_scale_depth, point_parabolic_speed=point_parabolic_speed)


def reference(thermal_loading, forcing_matrix, lagged_responses, pattern_heat_matrix, pattern_loading_matrix, starting_scale_depth, point_parabolic_speed):
    flipped = (lagged_responses[:, ::-1][:, None, :] * forcing_matrix.astype(jnp.float32)[:, :, None]).astype(jnp.bfloat16)
    padded = jnp.pad(thermal_loading, ((0, 0), (KERNEL - 1, 0)))
    modal_hist = lax.conv_general_dilated(padded[None].astype(jnp.float32), flipped.astype(jnp.float32), (1,), 'VALID', dimension_numbers=('NCH', 'OIH', 'NCH'), precision=lax.Precision.HIGHEST)[0]
    pattern_lines = lax.optimization_barrier(modal_hist.astype(jnp.bfloat16)).astype(jnp.float32).T
    bond_heat_excursion = jnp.dot(pattern_lines, pattern_heat_matrix.astype(jnp.float32), precision=lax.Precision.HIGHEST)
    bond_loading = jnp.dot(pattern_lines, pattern_loading_matrix.astype(jnp.float32), precision=lax.Precision.HIGHEST)
    layer_growth_amount = point_parabolic_speed[None, :] * jnp.exp(0.5 * bond_heat_excursion)
    grown_layer_depth = jnp.sqrt(starting_scale_depth[None, :] * starting_scale_depth[None, :] + 8.0 / TIME * jnp.cumsum(layer_growth_amount, axis=0))
    oxide_share = grown_layer_depth / (grown_layer_depth + 2.0)
    increment = jnp.square(bond_loading / (1.0 - 0.8 * oxide_share))
    fatigue_harm = jnp.cumsum(increment, axis=0) / TIME
    return (bond_heat_excursion, bond_loading, grown_layer_depth, fatigue_harm)
```

```python
import functools

import jax
import jax.numpy as jnp
from jax import lax
from jax.experimental import pallas as pl
from jax.experimental.pallas import tpu as pltpu
from jax.sharding import PartitionSpec as P

MESH = pl.DeviceIdType.MESH
F32, BF16 = jnp.float32, jnp.bfloat16
RING = 4
CORES = 2
HALF = 256
COLS = 256
NT = (((1,), (1,)), ((), ()))


def dot(a, b):
    return jnp.dot(a, b, preferred_element_type=F32)


def split_dot(tri, values):
    high = values.astype(BF16)
    low = (values - high.astype(F32)).astype(BF16)
    return dot(tri, high) + dot(tri, low)


def kernel(
    tms, line,
    x_in, f_in, r_in, hh_in, hl_in, s0_in, p_in,
    heat, load, depth, harm,
    x2, fv, rv, r2, hh, hl, s0, p, halo, ys, yh, part, g, lhs, tri, tot, mine, rec,
    in_sem, halo_sem, ssem, rsem, xs, xr,
):
    tm = lax.axis_index("tm")
    me = lax.axis_index("node")
    core = lax.rem(me, CORES)
    z = lax.rem(me // CORES, line)
    x = me // (CORES * line)
    modes = f_in.shape[0]
    points = heat.shape[1]
    tiles = points // COLS

    def node(x, z, c):
        return (x * line + z) * CORES + c

    right, left, across = lax.rem(x + 1, RING), lax.rem(x + 3, RING), lax.rem(x + 2, RING)
    sib = node(x, z, 1 - core)
    to_right, to_left = node(right, z, core), node(left, z, core)
    if line == 4:
        upper = z // 2
        others = (1 - z + 4 * upper, 2 - upper, 3 - 3 * upper)
    else:
        others = (1 - z,)
    column = (z, *others)

    loads = [
        pltpu.make_async_copy(a, b, in_sem.at[i])
        for i, (a, b) in enumerate((
            (f_in, fv),
            (x_in, x2.at[pl.ds(modes, modes), :]),
            (x_in.at[:, pl.ds(0, HALF)], x2.at[pl.ds(0, modes), pl.ds(HALF, HALF)]),
            (r_in, rv.at[pl.ds(0, modes), :]),
            (r_in, rv.at[pl.ds(modes, modes), :]),
            (s0_in, s0),
            (p_in, p),
            (hh_in, hh),
            (hl_in, hl),
        ))
    ]
    for copy in loads:
        copy.start()

    barrier = pltpu.get_barrier_semaphore()
    for other in (sib, to_right, to_left, *(node(x, o, core) for o in others)):
        pl.semaphore_signal(barrier, inc=1, device_id=(tm, other), device_id_type=MESH)
    for d in range(1, tms):
        pl.semaphore_signal(barrier, inc=1, device_id=(lax.rem(tm + d, tms), me), device_id_type=MESH)

    x2[pl.ds(0, modes), pl.ds(0, HALF)] = jnp.zeros((modes, HALF), BF16)
    tri[...] = (
        lax.broadcasted_iota(jnp.int32, (HALF, HALF), 0)
        >= lax.broadcasted_iota(jnp.int32, (HALF, HALF), 1)
    ).astype(F32).astype(BF16)
    for copy in loads[:5]:
        copy.wait()

    both = 2 * modes
    twice = (
        lax.rem(lax.broadcasted_iota(jnp.int32, (both, modes), 0), modes)
        == lax.broadcasted_iota(jnp.int32, (both, modes), 1)
    ).astype(F32).astype(BF16)
    wide = lax.dot_general(dot(twice, fv[...]).astype(BF16), twice, NT, preferred_element_type=F32)
    same = (
        lax.broadcasted_iota(jnp.int32, (both, both), 0) // modes
        == lax.broadcasted_iota(jnp.int32, (both, both), 1) // modes
    )
    drive = jnp.where(same, wide, 0.0).astype(BF16)

    def driven(source):
        return lax.dot_general(
            source.astype(F32).T.astype(BF16), drive, NT, preferred_element_type=F32
        )

    r2[...] = rv[...].T
    y = driven(x2[...])
    for s in range(8):
        ys[s] = y if s == 0 else pltpu.roll(y, s, 0)

    def lags(source, rows):
        def some(a, total):
            at = pl.multiple_of(HALF - 8 * a, 8)
            weights = r2[pl.ds(pl.multiple_of(8 * a, 8), 8), :]
            for s in range(8):
                total = total + weights[s : s + 1, :] * source[s, pl.ds(at, rows), :]
            return total

        return some

    local = lax.fori_loop(0, HALF // 8, lags(ys, HALF), jnp.zeros((HALF, both), F32)).T
    part[...] = local[:modes]
    g[0, me] = local[modes:].astype(BF16)

    pl.semaphore_wait(barrier, 3 + len(others) + tms - 1)

    def halo_copy():
        return pltpu.make_async_remote_copy(
            src_ref=x2.at[pl.ds(modes, modes), pl.ds(HALF, HALF)],
            dst_ref=halo,
            send_sem=halo_sem.at[0],
            recv_sem=halo_sem.at[1],
            device_id=(lax.rem(tm + 1, tms), me),
            device_id_type=MESH,
        )

    def block(q, of, to, i):
        return pltpu.make_async_remote_copy(
            src_ref=g.at[q, of],
            dst_ref=g.at[q, of],
            send_sem=ssem.at[q, i],
            recv_sem=rsem.at[q, of],
            device_id=(tm, to),
            device_id_type=MESH,
        )

    def arrived(q, of):
        block(q, of, sib, 0).wait_recv()

    sent = [0, 0]

    def send(q, of, to):
        block(q, of, to, sent[q]).start()
        sent[q] += 1

    def own(q):
        send(q, me, to_right)
        send(q, me, to_left)
        for o in others:
            send(q, me, node(x, o, core))
        send(q, me, sib)

    def along_line(q):
        for o in others:
            of = node(x, o, core)
            arrived(q, of)
            send(q, of, to_right)
            send(q, of, to_left)
            send(q, of, sib)

    def along_ring(q, o):
        a, b = node(left, o, core), node(right, o, core)
        even = 1 - lax.rem(o, 2)
        first = even * a + (1 - even) * b
        second = (1 - even) * a + even * b
        arrived(q, first)
        send(q, first, even * to_right + (1 - even) * to_left)
        send(q, first, sib)
        arrived(q, second)
        send(q, second, sib)

    def far_side(q, o):
        of = node(across, o, core)
        arrived(q, of)
        send(q, of, sib)

    def turn(q):
        for xs_ in (x, left, right, across):
            for o in column:
                chip = xs_ * line + o
                arrived(q, chip * CORES + 1 - core)
                both_cores = g[q, pl.ds(chip * CORES, CORES)].reshape(both, HALF)
                lhs[q, :, pl.ds(pl.multiple_of(chip * both, both), both)] = both_cores.T

    def rows(q):
        return pl.ds(HALF * (1 - q), HALF)

    def tile(j):
        return pl.ds(pl.multiple_of(j * COLS, COLS), COLS)

    def heat_tile(q, j):
        cols = tile(j)
        value = dot(lhs[q], hh[:, cols])
        heat[rows(q), cols] = value
        within = split_dot(tri[...], p[:, cols] * jnp.exp(0.5 * value))
        depth[rows(q), cols] = within
        tot[q, :, cols] = within[HALF - 1 :, :]

    def load_tile(q, j):
        cols = tile(j)
        load[rows(q), cols] = dot(lhs[q], hl[:, cols])

    @pl.when(tm + 1 < tms)
    def _():
        halo_copy().start()

    own(0)
    along_line(0)

    @pl.when(tm > 0)
    def _():
        halo_copy().wait_recv()

    @pl.when(tm == 0)
    def _():
        halo[...] = jnp.zeros_like(halo)

    before = halo[...]
    shifted = jnp.concatenate([before[:, both:], jnp.zeros((modes, HALF - both), BF16)], axis=1)
    y = driven(jnp.concatenate([before, shifted], axis=0))
    y = jnp.concatenate([y, jnp.zeros((64, both), F32)], axis=0)
    for s in range(8):
        yh[s] = y if s == 0 else pltpu.roll(y, s, 0)
    first = lax.fori_loop(0, 8, lags(yh, 64), jnp.zeros((64, both), F32))
    first = jnp.concatenate([first, jnp.zeros((both - 64, both), F32)], axis=0)
    late = lax.fori_loop(8, HALF // 8, lags(yh, both), first).T
    late = jnp.concatenate([late[:modes], late[modes:]], axis=1)
    g[1, me] = (part[...] + late).astype(BF16)

    own(1)
    for o in column:
        along_ring(0, o)
    along_line(1)
    for o in column:
        far_side(0, o)
    turn(0)
    for copy in loads[5:]:
        copy.wait()
    for j, o in enumerate(column):
        if j < tiles:
            heat_tile(0, j)
        along_ring(1, o)
    for j, o in enumerate(column):
        if j < tiles:
            load_tile(0, j)
        far_side(1, o)
    turn(1)

    def over(count, one):
        lax.fori_loop(0, count, lambda j, _: (one(j), None)[1], None)

    over(tiles, functools.partial(heat_tile, 1))

    def total_copy(stage, d):
        return pltpu.make_async_remote_copy(
            src_ref=mine.at[stage],
            dst_ref=rec.at[stage, tm],
            send_sem=xs.at[stage, d],
            recv_sem=xr.at[stage, tm],
            device_id=(lax.rem(tm + d, tms), me),
            device_id_type=MESH,
        )

    def give(stage):
        mine[stage] = tot[2 * stage] + tot[2 * stage + 1]
        for d in range(tms - 1, 0, -1):

            @pl.when(tm + d < tms)
            def _():
                total_copy(stage, d).start()

    def take(stage):
        def one(i, total):
            pltpu.make_async_remote_copy(
                src_ref=mine.at[stage],
                dst_ref=rec.at[stage, i],
                send_sem=xs.at[stage, 0],
                recv_sem=xr.at[stage, i],
                device_id=(lax.rem(tm + 1, tms), me),
                device_id_type=MESH,
            ).wait_recv()
            return total + rec[stage, i]

        return lax.fori_loop(0, tm, one, jnp.zeros((1, points), F32))

    give(0)
    over(tiles, functools.partial(load_tile, 1))
    share = 8.0 / (2 * HALF * tms)
    earlier = take(0)
    rec[0, tm] = s0[...] * s0[...] + share * earlier

    def depth_tile(q, j):
        cols = tile(j)
        base = rec[0, tm, :, cols]
        if q == 0:
            base = base + share * tot[1, :, cols]
        square = base + share * depth[rows(q), cols]
        layer = square * lax.rsqrt(square)
        depth[rows(q), cols] = layer
        stress = load[rows(q), cols] * (5.0 - 40.0 / (layer + 10.0))
        within = split_dot(tri[...], stress * stress)
        harm[rows(q), cols] = within
        tot[2 + q, :, cols] = within[HALF - 1 :, :]

    over(tiles, functools.partial(depth_tile, 1))
    over(tiles, functools.partial(depth_tile, 0))
    give(1)
    rec[1, tm] = take(1)

    def harm_tile(q, j):
        cols = tile(j)
        base = rec[1, tm, :, cols]
        if q == 0:
            base = base + tot[3, :, cols]
        harm[rows(q), cols] = (harm[rows(q), cols] + base) * (1.0 / (2 * HALF * tms))

    over(tiles, functools.partial(harm_tile, 1))
    over(tiles, functools.partial(harm_tile, 0))

    @pl.when(tm + 1 < tms)
    def _():
        halo_copy().wait_send()

    for stage in range(2):
        for d in range(1, tms):

            @pl.when(tm + d < tms)
            def _():
                total_copy(stage, d).wait_send()

    for q in range(2):
        for i in range(sent[q]):
            block(q, me, sib, i).wait_send()


def shards(tms, line, x, f, r, hh, hl, s0, p):
    modes, lags = r.shape
    steps = x.shape[1]
    points = hh.shape[1]
    nodes = RING * line * CORES
    every = nodes * modes
    hbm = pl.BlockSpec(memory_space=pltpu.HBM)
    vmem = pl.BlockSpec(memory_space=pltpu.VMEM)
    dma = pltpu.SemaphoreType.DMA
    sends = 2 + line - 1 + 1 + 3 * (line - 1) + 3 * line + line
    arrays = (x, f, r, hh, hl, s0.reshape(1, points), p.reshape(1, points))
    return pl.pallas_call(
        functools.partial(kernel, tms, line),
        out_shape=[pltpu.VMEM((steps, points), F32)] * 4,
        in_specs=[hbm] * 7,
        out_specs=[vmem] * 4,
        scratch_shapes=[
            pltpu.VMEM((2 * modes, steps), BF16),
            pltpu.VMEM(f.shape, BF16),
            pltpu.VMEM((2 * modes, lags), F32),
            pltpu.VMEM((lags, 2 * modes), F32),
            pltpu.VMEM(hh.shape, BF16),
            pltpu.VMEM(hl.shape, BF16),
            pltpu.VMEM((1, points), F32),
            pltpu.VMEM((1, points), F32),
            pltpu.VMEM((modes, HALF), BF16),
            pltpu.VMEM((8, steps, 2 * modes), F32),
            pltpu.VMEM((8, HALF + 64, 2 * modes), F32),
            pltpu.VMEM((modes, HALF), F32),
            pltpu.VMEM((2, nodes, modes, HALF), BF16),
            pltpu.VMEM((2, HALF, every), BF16),
            pltpu.VMEM((HALF, HALF), BF16),
            pltpu.VMEM((4, 1, points), F32),
            pltpu.VMEM((2, 1, points), F32),
            pltpu.VMEM((2, tms, 1, points), F32),
            dma((9,)),
            dma((2,)),
            dma((2, sends)),
            dma((2, nodes)),
            dma((2, tms)),
            dma((2, tms)),
        ],
        compiler_params=pltpu.CompilerParams(
            collective_id=0, has_side_effects=True, vmem_limit_bytes=40 * 1024 * 1024
        ),
    )(*(pltpu.with_memory_space_constraint(a, pltpu.HBM) for a in arrays))


def solution(mesh):
    tms, nodes = mesh.shape["tm"], mesh.shape["node"]
    return jax.shard_map(
        functools.partial(shards, tms, nodes // (RING * CORES)),
        mesh=mesh,
        in_specs=(
            P(None, "tm"),
            P("node", None),
            P("node", None),
            P(None, "node"),
            P(None, "node"),
            P("node"),
            P("node"),
        ),
        out_specs=(P("tm", "node"),) * 4,
        check_vma=False,
    )
```

```python
import functools

import jax
import jax.numpy as jnp
from jax import lax
from jax.experimental import pallas as pl
from jax.experimental.pallas import tpu as pltpu
from jax.sharding import PartitionSpec as P

MESH = pl.DeviceIdType.MESH
F32, BF16 = jnp.float32, jnp.bfloat16
RING = 4
CORES = 2
HALF = 256
COLS = 256
PIECES = 2
NT = (((1,), (1,)), ((), ()))


def dot(a, b):
    return jnp.dot(a, b, preferred_element_type=F32)


def split_dot(tri, values):
    high = values.astype(BF16)
    low = (values - high.astype(F32)).astype(BF16)
    return dot(tri, high) + dot(tri, low)


def kernel(
    tms, line,
    x_in, f_in, r_in, hh_in, hl_in, s0_in, p_in,
    heat, load, depth, harm,
    x2, fv, rv, r2, hh, hl, s0, p, halo, ys, yh, part, g, lhs, tri, tot, mine, rec,
    in_sem, halo_sem, ssem, rsem, bsem, xs, xr,
):
    tm = lax.axis_index("tm")
    me = lax.axis_index("node")
    core = lax.rem(me, CORES)
    z = lax.rem(me // CORES, line)
    x = me // (CORES * line)
    modes = f_in.shape[0]
    points = heat.shape[1]
    tiles = points // COLS

    def node(x, z, c):
        return (x * line + z) * CORES + c

    right, left, across = lax.rem(x + 1, RING), lax.rem(x + 3, RING), lax.rem(x + 2, RING)
    sib = node(x, z, 1 - core)
    others_x = (right, left, across)
    along_x = tuple(node(o, z, core) for o in others_x)
    if line == 4:
        upper = z // 2
        others = (1 - z + 4 * upper, 2 - upper, 3 - 3 * upper)
    else:
        others = (1 - z,)
    along_z = tuple(node(x, o, core) for o in others)
    near = [(x, z), *((x, o) for o in others), *((o, z) for o in others_x)]
    far = [(a, b) for b in others for a in others_x]
    chips = [a * line + b for a, b in near + far]
    both = CORES * modes

    loads = [
        pltpu.make_async_copy(a, b, in_sem.at[i])
        for i, (a, b) in enumerate((
            (f_in, fv),
            (x_in, x2.at[pl.ds(modes, modes), :]),
            (x_in.at[:, pl.ds(0, HALF)], x2.at[pl.ds(0, modes), pl.ds(HALF, HALF)]),
            (r_in, rv.at[pl.ds(0, modes), :]),
            (r_in, rv.at[pl.ds(modes, modes), :]),
            (s0_in, s0),
            (p_in, p),
        ))
    ]

    def pattern_loads(i):
        there = pl.ds(pl.multiple_of(chips[i] * both, both), both)
        here = pl.ds(i * both, both)
        return [
            pltpu.make_async_copy(a.at[there], b.at[here], in_sem.at[7 + 2 * i + k])
            for k, (a, b) in enumerate(((hh_in, hh), (hl_in, hl)))
        ]

    for copy in loads:
        copy.start()

    barrier = pltpu.get_barrier_semaphore()
    for other in (sib, *along_x, *along_z):
        pl.semaphore_signal(barrier, inc=1, device_id=(tm, other), device_id_type=MESH)
    for d in range(1, tms):
        pl.semaphore_signal(barrier, inc=1, device_id=(lax.rem(tm + d, tms), me), device_id_type=MESH)

    for i in range(len(chips)):
        for copy in pattern_loads(i):
            copy.start()
    x2[pl.ds(0, modes), pl.ds(0, HALF)] = jnp.zeros((modes, HALF), BF16)
    tri[...] = (
        lax.broadcasted_iota(jnp.int32, (HALF, HALF), 0)
        >= lax.broadcasted_iota(jnp.int32, (HALF, HALF), 1)
    ).astype(F32).astype(BF16)
    for copy in loads[:5]:
        copy.wait()

    twice = (
        lax.rem(lax.broadcasted_iota(jnp.int32, (both, modes), 0), modes)
        == lax.broadcasted_iota(jnp.int32, (both, modes), 1)
    ).astype(F32).astype(BF16)
    wide = lax.dot_general(dot(twice, fv[...]).astype(BF16), twice, NT, preferred_element_type=F32)
    same = (
        lax.broadcasted_iota(jnp.int32, (both, both), 0) // modes
        == lax.broadcasted_iota(jnp.int32, (both, both), 1) // modes
    )
    drive = jnp.where(same, wide, 0.0).astype(BF16)

    def driven(source):
        return lax.dot_general(
            source.astype(F32).T.astype(BF16), drive, NT, preferred_element_type=F32
        )

    r2[...] = rv[...].T
    y = driven(x2[...])
    for s in range(8):
        ys[s] = y if s == 0 else pltpu.roll(y, s, 0)

    def lags(source, rows):
        def some(a, total):
            at = pl.multiple_of(HALF - 8 * a, 8)
            weights = r2[pl.ds(pl.multiple_of(8 * a, 8), 8), :]
            for s in range(8):
                total = total + weights[s : s + 1, :] * source[s, pl.ds(at, rows), :]
            return total

        return some

    local = lax.fori_loop(0, HALF // 8, lags(ys, HALF), jnp.zeros((HALF, both), F32)).T
    part[...] = local[:modes]
    g[0, me] = local[modes:].astype(BF16)

    pl.semaphore_wait(barrier, 4 + len(others) + tms - 1)

    def halo_copy():
        return pltpu.make_async_remote_copy(
            src_ref=x2.at[pl.ds(modes, modes), pl.ds(HALF, HALF)],
            dst_ref=halo,
            send_sem=halo_sem.at[0],
            recv_sem=halo_sem.at[1],
            device_id=(lax.rem(tm + 1, tms), me),
            device_id_type=MESH,
        )

    cut = modes * 3 // 4
    whole, by_line, by_ring = (0, modes), (0, cut), (cut, modes - cut)

    def block(q, of, to, i, part):
        place = g.at[q, of, pl.ds(*part)]
        return pltpu.make_async_remote_copy(
            src_ref=place,
            dst_ref=place,
            send_sem=ssem.at[q, i],
            recv_sem=(bsem if part == by_ring else rsem).at[q, of],
            device_id=(tm, to),
            device_id_type=MESH,
        )

    def arrived(q, of, part):
        block(q, of, sib, 0, part).wait_recv()

    sent = [[], []]

    def send(q, of, to, part):
        block(q, of, to, len(sent[q]), part).start()
        sent[q].append(part)

    def own(q):
        order = (along_z[0], *along_x[:2], *along_z[1:], along_x[2], sib)
        for to in order:
            send(q, me, to, whole)

    def line_in(q, i):
        of = along_z[i]
        arrived(q, of, whole)
        for to in along_x:
            send(q, of, to, by_line)
        send(q, of, sib, whole)

    def ring_in(q, i):
        of = along_x[i]
        arrived(q, of, whole)
        for to in along_z:
            send(q, of, to, by_ring)
        send(q, of, sib, whole)

    def far_in(q, i):
        of = node(*far[i], core)
        arrived(q, of, by_line)
        arrived(q, of, by_ring)
        send(q, of, sib, whole)

    def turn(q, some):
        for i in some:
            arrived(q, chips[i] * CORES + 1 - core, whole)
            both_cores = g[q, pl.ds(chips[i] * CORES, CORES)].reshape(both, HALF)
            lhs[q, :, pl.ds(i * both, both)] = both_cores.T

    def rows(q):
        return pl.ds(HALF * (1 - q), HALF)

    def tile(j):
        return pl.ds(j * COLS, COLS)

    group = len(chips) // 2
    span = group * both

    def add_group(out, patterns, q, k):
        some = pl.ds(k * span, span)
        value = dot(lhs[q, :, some], patterns[some, :])
        out[rows(q), :] = value if k == 0 else out[rows(q), :] + value

    def grow(q):
        for j in range(tiles):
            cols = tile(j)
            growth = p[:, cols] * jnp.exp(0.5 * heat[rows(q), cols])
            within = split_dot(tri[...], growth)
            depth[rows(q), cols] = within
            tot[q, :, cols] = within[HALF - 1 :, :]

    @pl.when(tm + 1 < tms)
    def _():
        halo_copy().start()

    own(0)
    line_in(0, 0)
    ring_in(0, 0)
    ring_in(0, 1)

    @pl.when(tm > 0)
    def _():
        halo_copy().wait_recv()

    @pl.when(tm == 0)
    def _():
        halo[...] = jnp.zeros_like(halo)

    before = halo[...]
    shifted = jnp.concatenate([before[:, both:], jnp.zeros((modes, HALF - both), BF16)], axis=1)
    y = driven(jnp.concatenate([before, shifted], axis=0))
    y = jnp.concatenate([y, jnp.zeros((64, both), F32)], axis=0)
    for s in range(8):
        yh[s] = y if s == 0 else pltpu.roll(y, s, 0)
    first = lax.fori_loop(0, 8, lags(yh, 64), jnp.zeros((64, both), F32))
    first = jnp.concatenate([first, jnp.zeros((both - 64, both), F32)], axis=0)
    late = lax.fori_loop(8, HALF // 8, lags(yh, both), first).T
    late = jnp.concatenate([late[:modes], late[modes:]], axis=1)
    g[1, me] = (part[...] + late).astype(BF16)

    own(1)
    for i in range(1, len(others)):
        line_in(0, i)
    ring_in(0, 2)
    n_near, n_far = len(near), len(far)
    soon = 2 * n_far // 3
    turn(0, range(n_near))
    line_in(1, 0)
    ring_in(1, 0)
    ring_in(1, 1)
    for i in range(n_far // 2):
        far_in(0, i)
    turn(0, range(n_near, group))
    for copy in loads[5:]:
        copy.wait()
    for i in range(len(chips)):
        for copy in pattern_loads(i):
            copy.wait()
    add_group(heat, hh, 0, 0)
    for i in range(1, len(others)):
        line_in(1, i)
    ring_in(1, 2)
    for i in range(n_far // 2, n_far):
        far_in(0, i)
    add_group(load, hl, 0, 0)
    turn(0, range(max(n_near, group), n_near + n_far))
    add_group(heat, hh, 0, 1)
    for i in range(soon):
        far_in(1, i)
    turn(1, range(group))
    add_group(load, hl, 0, 1)
    grow(0)
    add_group(heat, hh, 1, 0)
    for i in range(soon, n_far):
        far_in(1, i)
    add_group(load, hl, 1, 0)
    turn(1, range(group, n_near + n_far))
    add_group(heat, hh, 1, 1)
    grow(1)

    def over(count, one):
        for j in range(count):
            one(j)

    def total_copy(stage, d):
        return pltpu.make_async_remote_copy(
            src_ref=mine.at[stage],
            dst_ref=rec.at[stage, tm],
            send_sem=xs.at[stage, d],
            recv_sem=xr.at[stage, tm],
            device_id=(lax.rem(tm + d, tms), me),
            device_id_type=MESH,
        )

    def give(stage):
        mine[stage] = tot[2 * stage] + tot[2 * stage + 1]
        for d in range(tms - 1, 0, -1):

            @pl.when(tm + d < tms)
            def _():
                total_copy(stage, d).start()

    def take(stage):
        def one(i, total):
            pltpu.make_async_remote_copy(
                src_ref=mine.at[stage],
                dst_ref=rec.at[stage, i],
                send_sem=xs.at[stage, 0],
                recv_sem=xr.at[stage, i],
                device_id=(lax.rem(tm + 1, tms), me),
                device_id_type=MESH,
            ).wait_recv()
            return total + rec[stage, i]

        return lax.fori_loop(0, tm, one, jnp.zeros((1, points), F32))

    give(0)
    add_group(load, hl, 1, 1)
    share = 8.0 / (2 * HALF * tms)
    earlier = take(0)
    rec[0, tm] = s0[...] * s0[...] + share * earlier

    def depth_tile(q, j):
        cols = tile(j)
        base = rec[0, tm, :, cols]
        if q == 0:
            base = base + share * tot[1, :, cols]
        square = base + share * depth[rows(q), cols]
        layer = square * lax.rsqrt(square)
        depth[rows(q), cols] = layer
        stress = load[rows(q), cols] * (5.0 - 40.0 / (layer + 10.0))
        within = split_dot(tri[...], stress * stress)
        harm[rows(q), cols] = within
        tot[2 + q, :, cols] = within[HALF - 1 :, :]

    over(tiles, functools.partial(depth_tile, 1))
    over(tiles, functools.partial(depth_tile, 0))
    give(1)
    rec[1, tm] = take(1)

    def harm_tile(q, j):
        cols = tile(j)
        base = rec[1, tm, :, cols]
        if q == 0:
            base = base + tot[3, :, cols]
        harm[rows(q), cols] = (harm[rows(q), cols] + base) * (1.0 / (2 * HALF * tms))

    over(tiles, functools.partial(harm_tile, 1))
    over(tiles, functools.partial(harm_tile, 0))

    @pl.when(tm + 1 < tms)
    def _():
        halo_copy().wait_send()

    for stage in range(2):
        for d in range(1, tms):

            @pl.when(tm + d < tms)
            def _():
                total_copy(stage, d).wait_send()

    for q in range(2):
        for i, part_sent in enumerate(sent[q]):
            block(q, me, sib, i, part_sent).wait_send()


def writer(*refs):
    sem = refs[8]
    size = refs[0].shape[0] // PIECES
    copies = [
        pltpu.make_async_copy(
            refs[i].at[pl.ds(k * size, size)], refs[4 + i].at[pl.ds(k * size, size)], sem.at[i, k]
        )
        for i in range(4)
        for k in range(PIECES)
    ]
    for copy in copies:
        copy.start()
    for copy in copies:
        copy.wait()


def shards(tms, line, x, f, r, hh, hl, s0, p):
    modes, lags = r.shape
    steps = x.shape[1]
    points = hh.shape[1]
    nodes = RING * line * CORES
    every = nodes * modes
    hbm = pl.BlockSpec(memory_space=pltpu.HBM)
    vmem = pl.BlockSpec(memory_space=pltpu.VMEM)
    dma = pltpu.SemaphoreType.DMA
    sends = (line + 3) + 4 * (line - 1) + 3 * line + 3 * (line - 1)
    arrays = (x, f, r, hh, hl, s0.reshape(1, points), p.reshape(1, points))
    results = pl.pallas_call(
        functools.partial(kernel, tms, line),
        out_shape=[pltpu.VMEM((steps, points), F32)] * 4,
        in_specs=[hbm] * 7,
        out_specs=[vmem] * 4,
        scratch_shapes=[
            pltpu.VMEM((2 * modes, steps), BF16),
            pltpu.VMEM(f.shape, BF16),
            pltpu.VMEM((2 * modes, lags), F32),
            pltpu.VMEM((lags, 2 * modes), F32),
            pltpu.VMEM(hh.shape, BF16),
            pltpu.VMEM(hl.shape, BF16),
            pltpu.VMEM((1, points), F32),
            pltpu.VMEM((1, points), F32),
            pltpu.VMEM((modes, HALF), BF16),
            pltpu.VMEM((8, steps, 2 * modes), F32),
            pltpu.VMEM((8, HALF + 64, 2 * modes), F32),
            pltpu.VMEM((modes, HALF), F32),
            pltpu.VMEM((2, nodes, modes, HALF), BF16),
            pltpu.VMEM((2, HALF, every), BF16),
            pltpu.VMEM((HALF, HALF), BF16),
            pltpu.VMEM((4, 1, points), F32),
            pltpu.VMEM((2, 1, points), F32),
            pltpu.VMEM((2, tms, 1, points), F32),
            dma((7 + 2 * RING * line,)),
            dma((2,)),
            dma((2, sends)),
            dma((2, nodes)),
            dma((2, nodes)),
            dma((2, tms)),
            dma((2, tms)),
        ],
        compiler_params=pltpu.CompilerParams(
            collective_id=0, has_side_effects=True, vmem_limit_bytes=40 * 1024 * 1024
        ),
    )(*(pltpu.with_memory_space_constraint(a, pltpu.HBM) for a in arrays))
    return pl.pallas_call(
        writer,
        out_shape=[jax.ShapeDtypeStruct((steps, points), F32)] * 4,
        in_specs=[vmem] * 4,
        out_specs=[pl.BlockSpec(memory_space=pl.ANY)] * 4,
        scratch_shapes=[dma((4, PIECES))],
        compiler_params=pltpu.CompilerParams(vmem_limit_bytes=4 * 1024 * 1024),
    )(*results)


def solution(mesh):
    tms, nodes = mesh.shape["tm"], mesh.shape["node"]
    return jax.shard_map(
        functools.partial(shards, tms, nodes // (RING * CORES)),
        mesh=mesh,
        in_specs=(
            P(None, "tm"),
            P("node", None),
            P("node", None),
            P(None, "node"),
            P(None, "node"),
            P("node"),
            P("node"),
        ),
        out_specs=(P("tm", "node"),) * 4,
        check_vma=False,
    )
```

```python
import functools

import jax
import jax.numpy as jnp
from jax import lax
from jax.experimental import pallas as pl
from jax.experimental.pallas import tpu as pltpu
from jax.sharding import PartitionSpec as P

MESH = pl.DeviceIdType.MESH
F32, BF16 = jnp.float32, jnp.bfloat16
RING = 4
CORES = 2
HALF = 256
COLS = 256
PIECES = 2
NT = (((1,), (1,)), ((), ()))


def dot(a, b):
    return jnp.dot(a, b, preferred_element_type=F32)


def split_dot(tri, values):
    high = values.astype(BF16)
    low = (values - high.astype(F32)).astype(BF16)
    return dot(tri, high) + dot(tri, low)


def kernel(
    tms, line,
    x_in, f_in, r_in, hh_in, hl_in, s0_in, p_in,
    heat, load, depth, harm,
    x2, fv, rv, r2, hh, hl, s0, p, halo, ys, yh, g, lhs, tri, tot, mine, rec,
    in_sem, halo_sem, ssem, rsem, bsem, xs, xr, ready,
):
    tm = lax.axis_index("tm")
    me = lax.axis_index("node")
    core = lax.rem(me, CORES)
    z = lax.rem(me // CORES, line)
    x = me // (CORES * line)
    modes = f_in.shape[0]
    points = heat.shape[1]
    tiles = points // COLS

    def node(x, z, c):
        return (x * line + z) * CORES + c

    right, left, across = lax.rem(x + 1, RING), lax.rem(x + 3, RING), lax.rem(x + 2, RING)
    sib = node(x, z, 1 - core)
    others_x = (right, left, across)
    along_x = tuple(node(o, z, core) for o in others_x)
    if line == 4:
        upper = z // 2
        others = (1 - z + 4 * upper, 2 - upper, 3 - 3 * upper)
    else:
        others = (1 - z,)
    along_z = tuple(node(x, o, core) for o in others)
    columns = (x, *others_x)
    chips = [a * line + b for a in columns for b in range(line)]
    both = CORES * modes

    loads = [
        pltpu.make_async_copy(a, b, in_sem.at[i])
        for i, (a, b) in enumerate((
            (f_in, fv),
            (x_in, x2.at[pl.ds(modes, modes), :]),
            (x_in.at[:, pl.ds(0, HALF)], x2.at[pl.ds(0, modes), pl.ds(HALF, HALF)]),
            (r_in, rv.at[pl.ds(0, modes), :]),
            (r_in, rv.at[pl.ds(modes, modes), :]),
            (s0_in, s0),
            (p_in, p),
        ))
    ]

    def pattern_loads(i):
        there = pl.ds(pl.multiple_of(chips[i] * both, both), both)
        here = pl.ds(i * both, both)
        return [
            pltpu.make_async_copy(a.at[there], b.at[here], in_sem.at[7 + 2 * i + k])
            for k, (a, b) in enumerate(((hh_in, hh), (hl_in, hl)))
        ]

    for copy in loads:
        copy.start()

    barrier = pltpu.get_barrier_semaphore()
    for other in (sib, *along_x, *along_z):
        pl.semaphore_signal(barrier, inc=1, device_id=(tm, other), device_id_type=MESH)
    for d in range(1, tms):

        @pl.when(tm + d < tms)
        def _():
            pl.semaphore_signal(barrier, inc=1, device_id=(tm + d, me), device_id_type=MESH)

    @pl.when(tm > 0)
    def _():
        pl.semaphore_signal(barrier, inc=1, device_id=(tm - 1, me), device_id_type=MESH)


    for i in range(len(chips)):
        for copy in pattern_loads(i):
            copy.start()
    x2[pl.ds(0, modes), pl.ds(0, HALF)] = jnp.zeros((modes, HALF), BF16)
    tri[...] = (
        lax.broadcasted_iota(jnp.int32, (HALF, HALF), 0)
        >= lax.broadcasted_iota(jnp.int32, (HALF, HALF), 1)
    ).astype(F32).astype(BF16)
    for copy in loads[:5]:
        copy.wait()

    twice = (
        lax.rem(lax.broadcasted_iota(jnp.int32, (both, modes), 0), modes)
        == lax.broadcasted_iota(jnp.int32, (both, modes), 1)
    ).astype(F32).astype(BF16)
    wide = lax.dot_general(dot(twice, fv[...]).astype(BF16), twice, NT, preferred_element_type=F32)
    same = (
        lax.broadcasted_iota(jnp.int32, (both, both), 0) // modes
        == lax.broadcasted_iota(jnp.int32, (both, both), 1) // modes
    )
    drive = jnp.where(same, wide, 0.0).astype(BF16)

    def driven(source):
        return lax.dot_general(
            source.astype(F32).T.astype(BF16), drive, NT, preferred_element_type=F32
        )

    r2[...] = rv[...].T
    y = driven(x2[...])
    for s in range(8):
        ys[s] = y if s == 0 else pltpu.roll(y, s, 0)

    def lags(source, rows):
        def some(a, total):
            at = pl.multiple_of(HALF - 8 * a, 8)
            weights = r2[pl.ds(pl.multiple_of(8 * a, 8), 8), :]
            for s in range(8):
                total = total + weights[s : s + 1, :] * source[s, pl.ds(at, rows), :]
            return total

        return some

    groups = HALF // 8
    local = lax.fori_loop(0, groups // 2, lags(ys, HALF), jnp.zeros((HALF, both), F32))

    pl.semaphore_wait(barrier, 4 + len(others) + tm + 1 - (tm + 1) // tms)

    def halo_copy():
        return pltpu.make_async_remote_copy(
            src_ref=x2.at[pl.ds(modes, modes), pl.ds(HALF, HALF)],
            dst_ref=halo,
            send_sem=halo_sem.at[0],
            recv_sem=halo_sem.at[1],
            device_id=(lax.rem(tm + 1, tms), me),
            device_id_type=MESH,
        )

    def block(q, a, b, to, i):
        place = g.at[q, core, a, b]
        return pltpu.make_async_remote_copy(
            src_ref=place,
            dst_ref=place,
            send_sem=ssem.at[q, i],
            recv_sem=rsem.at[q, a * line + b],
            device_id=(tm, to),
            device_id_type=MESH,
        )

    def whole(q, a, c, i):
        place = g.at[q, c, a]
        return pltpu.make_async_remote_copy(
            src_ref=place,
            dst_ref=place,
            send_sem=bsem.at[0, q, i],
            recv_sem=bsem.at[1, q, a],
            device_id=(tm, sib),
            device_id_type=MESH,
        )

    def arrived(q, a, b):
        block(q, a, b, sib, 0).wait_recv()

    sent = [0, 0]

    def send(q, a, b, to):
        block(q, a, b, to, sent[q]).start()
        sent[q] += 1

    def own(q):
        for to in (*along_z[1:], *along_x[:2], along_z[0], along_x[2]):
            send(q, x, z, to)

    def line_in(q, i):
        arrived(q, x, others[i])
        if i > 0:
            for to in along_x:
                send(q, x, others[i], to)

    def ring_in(q, i):
        arrived(q, others_x[i], z)
        send(q, others_x[i], z, along_z[0])

    def near_in(q):
        for i in range(1, len(others)):
            line_in(q, i)
            ring_in(q, i - 1)
        for i in range(len(others) - 1, 3):
            ring_in(q, i)
        line_in(q, 0)
        whole(q, x, core, 0).start()

    def far_in(q, i):
        for b in others:
            arrived(q, columns[i], b)
        whole(q, columns[i], core, i).start()

    def turn(q, i):
        whole(q, columns[i], 1 - core, i).wait_recv()
        for b in range(line):
            pair = g[q, :, columns[i], b].reshape(both, HALF)
            lhs[q, :, pl.ds((i * line + b) * both, both)] = pair.T

    def rows(q):
        return pl.ds(HALF * (1 - q), HALF)

    def tile(j):
        return pl.ds(j * COLS, COLS)

    span = line * both

    def add_columns(out, patterns, q, first, count):
        some = pl.ds(first * span, count * span)
        value = dot(lhs[q, :, some], patterns[some, :])
        out[rows(q), :] = value if first == 0 else out[rows(q), :] + value

    def grow(q):
        for j in range(tiles):
            cols = tile(j)
            growth = p[:, cols] * jnp.exp(0.5 * heat[rows(q), cols])
            depth[rows(q), cols] = growth
            tot[q, :, cols] = jnp.sum(growth, axis=0, keepdims=True)

    def run_up(out, q):
        for j in range(tiles):
            cols = tile(j)
            out[rows(q), cols] = split_dot(tri[...], out[rows(q), cols])

    @pl.when(tm + 1 < tms)
    def _():
        halo_copy().start()

    for d in range(1, tms):

        @pl.when(tm >= d)
        def _():
            pl.semaphore_signal(ready, inc=1, device_id=(tm - d, me), device_id_type=MESH)

    local = lax.fori_loop(groups // 2, groups, lags(ys, HALF), local).T
    part = local[:modes]
    g[0, core, x, z] = local[modes:].astype(BF16)
    own(0)

    @pl.when(tm > 0)
    def _():
        halo_copy().wait_recv()

    @pl.when(tm == 0)
    def _():
        halo[...] = jnp.zeros_like(halo)

    before = halo[...]
    shifted = jnp.concatenate([before[:, both:], jnp.zeros((modes, HALF - both), BF16)], axis=1)
    y = driven(jnp.concatenate([before, shifted], axis=0))
    y = jnp.concatenate([y, jnp.zeros((64, both), F32)], axis=0)
    for s in range(8):
        yh[s] = y if s == 0 else pltpu.roll(y, s, 0)
    first = lax.fori_loop(0, 8, lags(yh, 64), jnp.zeros((64, both), F32))
    first = jnp.concatenate([first, jnp.zeros((both - 64, both), F32)], axis=0)
    late = lax.fori_loop(8, groups, lags(yh, both), first).T
    late = jnp.concatenate([late[:modes], late[modes:]], axis=1)
    g[1, core, x, z] = (part + late).astype(BF16)

    own(1)
    near_in(0)
    turn(0, 0)
    for copy in loads[5:]:
        copy.wait()
    for i in range(len(chips)):
        for copy in pattern_loads(i):
            copy.wait()
    add_columns(heat, hh, 0, 0, 1)
    add_columns(load, hl, 0, 0, 1)
    near_in(1)
    far_in(0, 1)
    far_in(0, 2)
    turn(1, 0)
    add_columns(heat, hh, 1, 0, 1)
    add_columns(load, hl, 1, 0, 1)
    far_in(0, 3)
    turn(0, 1)
    turn(0, 2)
    add_columns(heat, hh, 0, 1, 2)
    add_columns(load, hl, 0, 1, 2)
    far_in(1, 1)
    far_in(1, 2)
    turn(0, 3)
    add_columns(heat, hh, 0, 3, 1)
    grow(0)
    far_in(1, 3)
    add_columns(load, hl, 0, 3, 1)
    turn(1, 1)
    turn(1, 2)
    add_columns(heat, hh, 1, 1, 2)
    add_columns(load, hl, 1, 1, 2)
    turn(1, 3)
    add_columns(heat, hh, 1, 3, 1)
    grow(1)

    def over(count, one):
        for j in range(count):
            one(j)

    def total_copy(stage, d):
        return pltpu.make_async_remote_copy(
            src_ref=mine.at[stage],
            dst_ref=rec.at[stage, tm],
            send_sem=xs.at[stage, d],
            recv_sem=xr.at[stage, tm],
            device_id=(lax.rem(tm + d, tms), me),
            device_id_type=MESH,
        )

    def give(stage):
        mine[stage] = tot[2 * stage] + tot[2 * stage + 1]
        for d in range(tms - 1, 0, -1):

            @pl.when(tm + d < tms)
            def _():
                total_copy(stage, d).start()

    def take(stage):
        def one(i, total):
            pltpu.make_async_remote_copy(
                src_ref=mine.at[stage],
                dst_ref=rec.at[stage, i],
                send_sem=xs.at[stage, 0],
                recv_sem=xr.at[stage, i],
                device_id=(lax.rem(tm + 1, tms), me),
                device_id_type=MESH,
            ).wait_recv()
            return total + rec[stage, i]

        return lax.fori_loop(0, tm, one, jnp.zeros((1, points), F32))


    @pl.when(tm + 1 < tms)
    def _():
        pl.semaphore_wait(ready, tms - 1 - tm)

    give(0)
    add_columns(load, hl, 1, 3, 1)
    run_up(depth, 1)
    run_up(depth, 0)
    share = 8.0 / (2 * HALF * tms)
    earlier = take(0)
    rec[0, tm] = s0[...] * s0[...] + share * earlier

    def depth_tile(q, j):
        cols = tile(j)
        base = rec[0, tm, :, cols]
        if q == 0:
            base = base + share * tot[1, :, cols]
        square = base + share * depth[rows(q), cols]
        layer = square * lax.rsqrt(square)
        depth[rows(q), cols] = layer
        stress = load[rows(q), cols] * (5.0 - 40.0 / (layer + 10.0))
        increment = stress * stress
        harm[rows(q), cols] = increment
        tot[2 + q, :, cols] = jnp.sum(increment, axis=0, keepdims=True)

    over(tiles, functools.partial(depth_tile, 1))
    over(tiles, functools.partial(depth_tile, 0))
    give(1)
    run_up(harm, 1)
    run_up(harm, 0)
    rec[1, tm] = take(1)

    def harm_tile(q, j):
        cols = tile(j)
        base = rec[1, tm, :, cols]
        if q == 0:
            base = base + tot[3, :, cols]
        harm[rows(q), cols] = (harm[rows(q), cols] + base) * (1.0 / (2 * HALF * tms))

    over(tiles, functools.partial(harm_tile, 1))
    over(tiles, functools.partial(harm_tile, 0))

    @pl.when(tm + 1 < tms)
    def _():
        halo_copy().wait_send()

    for stage in range(2):
        for d in range(1, tms):

            @pl.when(tm + d < tms)
            def _():
                total_copy(stage, d).wait_send()

    for q in range(2):
        for i in range(sent[q]):
            block(q, x, z, sib, i).wait_send()
        for i in range(RING):
            whole(q, x, core, i).wait_send()


def writer(*refs):
    sem = refs[8]
    size = refs[0].shape[0] // PIECES
    copies = [
        pltpu.make_async_copy(
            refs[i].at[pl.ds(k * size, size)], refs[4 + i].at[pl.ds(k * size, size)], sem.at[i, k]
        )
        for i in range(4)
        for k in range(PIECES)
    ]
    for copy in copies:
        copy.start()
    for copy in copies:
        copy.wait()


def shards(tms, line, x, f, r, hh, hl, s0, p):
    modes, lags = r.shape
    steps = x.shape[1]
    points = hh.shape[1]
    nodes = RING * line * CORES
    every = nodes * modes
    hbm = pl.BlockSpec(memory_space=pltpu.HBM)
    vmem = pl.BlockSpec(memory_space=pltpu.VMEM)
    dma = pltpu.SemaphoreType.DMA
    sends = (line + 2) + 3 + 3 * (line - 2)
    arrays = (x, f, r, hh, hl, s0.reshape(1, points), p.reshape(1, points))
    results = pl.pallas_call(
        functools.partial(kernel, tms, line),
        out_shape=[pltpu.VMEM((steps, points), F32)] * 4,
        in_specs=[hbm] * 7,
        out_specs=[vmem] * 4,
        scratch_shapes=[
            pltpu.VMEM((2 * modes, steps), BF16),
            pltpu.VMEM(f.shape, BF16),
            pltpu.VMEM((2 * modes, lags), F32),
            pltpu.VMEM((lags, 2 * modes), F32),
            pltpu.VMEM(hh.shape, BF16),
            pltpu.VMEM(hl.shape, BF16),
            pltpu.VMEM((1, points), F32),
            pltpu.VMEM((1, points), F32),
            pltpu.VMEM((modes, HALF), BF16),
            pltpu.VMEM((8, steps, 2 * modes), F32),
            pltpu.VMEM((8, HALF + 64, 2 * modes), F32),
            pltpu.VMEM((2, CORES, RING, line, modes, HALF), BF16),
            pltpu.VMEM((2, HALF, every), BF16),
            pltpu.VMEM((HALF, HALF), BF16),
            pltpu.VMEM((4, 1, points), F32),
            pltpu.VMEM((2, 1, points), F32),
            pltpu.VMEM((2, tms, 1, points), F32),
            dma((7 + 2 * RING * line,)),
            dma((2,)),
            dma((2, sends)),
            dma((2, RING * line)),
            dma((2, 2, RING)),
            dma((2, tms)),
            dma((2, tms)),
            pltpu.SemaphoreType.REGULAR,
        ],
        compiler_params=pltpu.CompilerParams(
            collective_id=0, has_side_effects=True, vmem_limit_bytes=40 * 1024 * 1024
        ),
    )(*(pltpu.with_memory_space_constraint(a, pltpu.HBM) for a in arrays))
    return pl.pallas_call(
        writer,
        out_shape=[jax.ShapeDtypeStruct((steps, points), F32)] * 4,
        in_specs=[vmem] * 4,
        out_specs=[pl.BlockSpec(memory_space=pl.ANY)] * 4,
        scratch_shapes=[dma((4, PIECES))],
        compiler_params=pltpu.CompilerParams(vmem_limit_bytes=4 * 1024 * 1024),
    )(*results)


def solution(mesh):
    tms, nodes = mesh.shape["tm"], mesh.shape["node"]
    return jax.shard_map(
        functools.partial(shards, tms, nodes // (RING * CORES)),
        mesh=mesh,
        in_specs=(
            P(None, "tm"),
            P("node", None),
            P("node", None),
            P(None, "node"),
            P(None, "node"),
            P("node"),
            P("node"),
        ),
        out_specs=(P("tm", "node"),) * 4,
        check_vma=False,
    )
```

```python
import functools

import jax
import jax.numpy as jnp
from jax import lax
from jax.experimental import pallas as pl
from jax.experimental.pallas import tpu as pltpu
from jax.sharding import PartitionSpec as P

MESH = pl.DeviceIdType.MESH
F32, BF16 = jnp.float32, jnp.bfloat16
RING = 4
CORES = 2
HALF = 256
COLS = 256
PIECES = 2
NT = (((1,), (1,)), ((), ()))


def dot(a, b):
    return jnp.dot(a, b, preferred_element_type=F32)


def split_dot(tri, values):
    high = values.astype(BF16)
    low = (values - high.astype(F32)).astype(BF16)
    return dot(tri, high) + dot(tri, low)


def kernel(
    tms, line,
    x_in, f_in, r_in, hh_in, hl_in, s0_in, p_in,
    heat, load, depth, harm, base,
    x2, fv, rv, r2, hh, hl, s0, p, halo, ys, yh, g, lhs, tri, tot, mine, rec,
    in_sem, halo_sem, ssem, rsem, bsem, xs, xr, ready,
):
    tm = lax.axis_index("tm")
    me = lax.axis_index("node")
    core = lax.rem(me, CORES)
    z = lax.rem(me // CORES, line)
    x = me // (CORES * line)
    modes = f_in.shape[0]
    points = heat.shape[1]
    tiles = points // COLS

    def node(x, z, c):
        return (x * line + z) * CORES + c

    right, left, across = lax.rem(x + 1, RING), lax.rem(x + 3, RING), lax.rem(x + 2, RING)
    sib = node(x, z, 1 - core)
    others_x = (right, left, across)
    along_x = tuple(node(o, z, core) for o in others_x)
    if line == 4:
        upper = z // 2
        beside = 1 - z + 4 * upper
        others = (beside, lax.rem(z + 2, line), lax.rem(beside + 2, line))
    else:
        others = (1 - z,)
    along_z = tuple(node(x, o, core) for o in others)
    columns = (x, *others_x)
    chips = [a * line + b for a in columns for b in range(line)]
    both = CORES * modes

    barrier = pltpu.get_barrier_semaphore()

    span = tms // 2
    mid = line // 2
    crossed_in = 1 - lax.min(1, lax.rem(tm, span))
    crossed_out = 1 - lax.min(1, lax.rem(tm + 1, span))
    at_end = 1 - lax.min(1, lax.rem(z, line - 1))
    nearer = (line - 1) * (1 - z // mid)
    server = node(x, z + crossed_in * (nearer - z), core)
    served = (1 - (tm + 1) // tms) * (1 - crossed_out + crossed_out * at_end * mid)

    @pl.when(tm > 0)
    def _():
        pl.semaphore_signal(barrier, inc=1, device_id=(tm - 1, server), device_id_type=MESH)


    for d in range(1, tms):

        @pl.when(tm + d < tms)
        def _():
            pl.semaphore_signal(barrier, inc=1, device_id=(tm + d, me), device_id_type=MESH)

    for other in (sib, *along_x, *along_z):
        pl.semaphore_signal(barrier, inc=1, device_id=(tm, other), device_id_type=MESH)

    loads = [
        pltpu.make_async_copy(a, b, in_sem.at[i])
        for i, (a, b) in enumerate((
            (f_in, fv),
            (x_in, x2.at[pl.ds(modes, modes), :]),
            (x_in.at[:, pl.ds(0, HALF)], x2.at[pl.ds(0, modes), pl.ds(HALF, HALF)]),
            (r_in, rv.at[pl.ds(0, modes), :]),
            (r_in, rv.at[pl.ds(modes, modes), :]),
            (s0_in, s0),
            (p_in, p),
        ))
    ]

    def pattern_loads(i):
        there = pl.ds(pl.multiple_of(chips[i] * both, both), both)
        here = pl.ds(i * both, both)
        return [
            pltpu.make_async_copy(a.at[there], b.at[here], in_sem.at[7 + 2 * i + k])
            for k, (a, b) in enumerate(((hh_in, hh), (hl_in, hl)))
        ]

    for copy in loads:
        copy.start()
    for i in range(len(chips)):
        for copy in pattern_loads(i):
            copy.start()
    x2[pl.ds(0, modes), pl.ds(0, HALF)] = jnp.zeros((modes, HALF), BF16)
    tri[...] = (
        lax.broadcasted_iota(jnp.int32, (HALF, HALF), 0)
        >= lax.broadcasted_iota(jnp.int32, (HALF, HALF), 1)
    ).astype(F32).astype(BF16)
    for copy in loads[:5]:
        copy.wait()

    twice = (
        lax.rem(lax.broadcasted_iota(jnp.int32, (both, modes), 0), modes)
        == lax.broadcasted_iota(jnp.int32, (both, modes), 1)
    ).astype(F32).astype(BF16)
    wide = lax.dot_general(dot(twice, fv[...]).astype(BF16), twice, NT, preferred_element_type=F32)
    same = (
        lax.broadcasted_iota(jnp.int32, (both, both), 0) // modes
        == lax.broadcasted_iota(jnp.int32, (both, both), 1) // modes
    )
    drive = jnp.where(same, wide, 0.0).astype(BF16)

    def driven(source):
        return lax.dot_general(
            source.astype(F32).T.astype(BF16), drive, NT, preferred_element_type=F32
        )

    r2[...] = rv[...].T
    y = driven(x2[...])
    for s in range(8):
        ys[s] = y if s == 0 else pltpu.roll(y, s, 0)

    def lags(source, rows):
        def some(a, total):
            at = pl.multiple_of(HALF - 8 * a, 8)
            weights = r2[pl.ds(pl.multiple_of(8 * a, 8), 8), :]
            for s in range(8):
                total = total + weights[s : s + 1, :] * source[s, pl.ds(at, rows), :]
            return total

        return some

    groups = HALF // 8
    turns = groups // 2 + groups // 2 * lax.min(1, tm // span)
    local = lax.fori_loop(0, turns, lags(ys, HALF), jnp.zeros((HALF, both), F32))

    pl.semaphore_wait(barrier, 4 + len(others) + tm + served)

    def halo_copy(i):
        there = z + crossed_out * (i + mid * (1 - lax.min(1, z)) - z)
        return pltpu.make_async_remote_copy(
            src_ref=x2.at[pl.ds(modes, modes), pl.ds(HALF, HALF)],
            dst_ref=halo,
            send_sem=halo_sem.at[i],
            recv_sem=halo_sem.at[mid],
            device_id=(lax.rem(tm + 1, tms), node(x, there, core)),
            device_id_type=MESH,
        )

    def block(q, a, b, to, i):
        place = g.at[q, core, a, b]
        return pltpu.make_async_remote_copy(
            src_ref=place,
            dst_ref=place,
            send_sem=ssem.at[q, i],
            recv_sem=rsem.at[q, a * line + b],
            device_id=(tm, to),
            device_id_type=MESH,
        )

    def whole(q, a, c, i):
        place = g.at[q, c, a]
        return pltpu.make_async_remote_copy(
            src_ref=place,
            dst_ref=place,
            send_sem=bsem.at[0, q, i],
            recv_sem=bsem.at[1, q, a],
            device_id=(tm, sib),
            device_id_type=MESH,
        )

    def arrived(q, a, b):
        block(q, a, b, sib, 0).wait_recv()

    sent = [0, 0]

    def send(q, a, b, to):
        block(q, a, b, to, sent[q]).start()
        sent[q] += 1

    def own(q):
        for to in (*along_z[1:], *along_x[::-1], along_z[0]):
            send(q, x, z, to)

    def line_in(q, i):
        arrived(q, x, others[i])
        if i > 0:
            for to in along_x[::-1]:
                send(q, x, others[i], to)

    def ring_in(q, i):
        arrived(q, others_x[i], z)
        send(q, others_x[i], z, along_z[0])

    def near_in():
        for q in range(2):
            for i in range(1, len(others)):
                line_in(q, i)
            for i in range(3):
                ring_in(q, i)
        for q in range(2):
            line_in(q, 0)
            whole(q, x, core, 0).start()

    def far_in(q, i):
        for b in others:
            arrived(q, columns[i], b)
        whole(q, columns[i], core, i).start()

    def turn(q, i):
        whole(q, columns[i], 1 - core, i).wait_recv()
        for b in range(line):
            pair = g[q, :, columns[i], b].reshape(both, HALF)
            lhs[q, :, pl.ds((i * line + b) * both, both)] = pair.T

    def rows(q):
        return pl.ds(HALF * (1 - q), HALF)

    def tile(j):
        return pl.ds(j * COLS, COLS)

    span = line * both

    def add_columns(out, patterns, q, first, count):
        some = pl.ds(first * span, count * span)
        value = dot(lhs[q, :, some], patterns[some, :])
        out[rows(q), :] = value if first == 0 else out[rows(q), :] + value

    def grow(q):
        for j in range(tiles):
            cols = tile(j)
            growth = p[:, cols] * jnp.exp(0.5 * heat[rows(q), cols])
            depth[rows(q), cols] = growth
            tot[q, :, cols] = jnp.sum(growth, axis=0, keepdims=True)

    def run_up(out, q):
        for j in range(tiles):
            cols = tile(j)
            out[rows(q), cols] = split_dot(tri[...], out[rows(q), cols])

    for i in range(mid):

        @pl.when(served > i)
        def _():
            halo_copy(i).start()

    for d in range(1, tms):

        @pl.when(tm >= d)
        def _():
            pl.semaphore_signal(ready, inc=1, device_id=(tm - d, me), device_id_type=MESH)

    local = lax.fori_loop(turns, groups, lags(ys, HALF), local).T
    part = local[:modes]
    g[0, core, x, z] = local[modes:].astype(BF16)
    own(0)

    @pl.when(tm > 0)
    def _():
        halo_copy(0).wait_recv()

    @pl.when(tm == 0)
    def _():
        halo[...] = jnp.zeros_like(halo)

    before = halo[...]
    shifted = jnp.concatenate([before[:, both:], jnp.zeros((modes, HALF - both), BF16)], axis=1)
    y = driven(jnp.concatenate([before, shifted], axis=0))
    y = jnp.concatenate([y, jnp.zeros((64, both), F32)], axis=0)
    for s in range(8):
        yh[s] = y if s == 0 else pltpu.roll(y, s, 0)
    first = lax.fori_loop(0, 8, lags(yh, 64), jnp.zeros((64, both), F32))
    first = jnp.concatenate([first, jnp.zeros((both - 64, both), F32)], axis=0)
    late = lax.fori_loop(8, groups, lags(yh, both), first).T
    late = jnp.concatenate([late[:modes], late[modes:]], axis=1)
    g[1, core, x, z] = (part + late).astype(BF16)

    own(1)
    near_in()
    turn(0, 0)
    for copy in loads[5:]:
        copy.wait()
    for i in range(len(chips)):
        for copy in pattern_loads(i):
            copy.wait()
    rest = RING - 1
    add_columns(heat, hh, 0, 0, 1)
    add_columns(load, hl, 0, 0, 1)
    turn(1, 0)
    add_columns(heat, hh, 1, 0, 1)
    for i in range(1, RING):
        far_in(0, i)
    add_columns(load, hl, 1, 0, 1)
    for i in range(1, RING):
        turn(0, i)
    add_columns(heat, hh, 0, 1, rest)
    grow(0)
    for i in range(1, RING):
        far_in(1, i)
    add_columns(load, hl, 0, 1, rest)
    for i in range(1, RING):
        turn(1, i)
    add_columns(heat, hh, 1, 1, rest)
    grow(1)

    def over(count, one):
        for j in range(count):
            one(j)

    def total_copy(stage, d):
        return pltpu.make_async_remote_copy(
            src_ref=mine.at[stage],
            dst_ref=rec.at[stage, tm],
            send_sem=xs.at[stage, d],
            recv_sem=xr.at[stage, tm],
            device_id=(lax.rem(tm + d, tms), me),
            device_id_type=MESH,
        )

    def give(stage):
        mine[stage] = tot[2 * stage] + tot[2 * stage + 1]
        for d in range(tms - 1, 0, -1):

            @pl.when(tm + d < tms)
            def _():
                total_copy(stage, d).start()

    def take(stage):
        def one(i, total):
            pltpu.make_async_remote_copy(
                src_ref=mine.at[stage],
                dst_ref=rec.at[stage, i],
                send_sem=xs.at[stage, 0],
                recv_sem=xr.at[stage, i],
                device_id=(lax.rem(tm + 1, tms), me),
                device_id_type=MESH,
            ).wait_recv()
            return total + rec[stage, i]

        return lax.fori_loop(0, tm, one, jnp.zeros((1, points), F32))


    @pl.when(tm + 1 < tms)
    def _():
        pl.semaphore_wait(ready, tms - 1 - tm)

    give(0)
    add_columns(load, hl, 1, 1, rest)
    run_up(depth, 1)
    run_up(depth, 0)

    for i in range(mid):

        @pl.when(served > i)
        def _():
            halo_copy(i).wait_send()

    for q in range(2):
        for i in range(sent[q]):
            block(q, x, z, sib, i).wait_send()
        for i in range(RING):
            whole(q, x, core, i).wait_send()

    share = 8.0 / (2 * HALF * tms)
    earlier = take(0)
    rec[0, tm] = s0[...] * s0[...] + share * earlier

    def depth_tile(q, j):
        cols = tile(j)
        start = rec[0, tm, :, cols]
        if q == 0:
            start = start + share * tot[1, :, cols]
        square = start + share * depth[rows(q), cols]
        layer = square * lax.rsqrt(square)
        depth[rows(q), cols] = layer
        stress = load[rows(q), cols] * (5.0 - 40.0 / (layer + 10.0))
        increment = stress * stress
        harm[rows(q), cols] = increment
        tot[2 + q, :, cols] = jnp.sum(increment, axis=0, keepdims=True)

    over(tiles, functools.partial(depth_tile, 1))
    over(tiles, functools.partial(depth_tile, 0))
    give(1)
    run_up(harm, 1)
    run_up(harm, 0)
    rec[1, tm] = take(1)

    base[0] = rec[1, tm]
    base[1] = rec[1, tm] + tot[3]

    for stage in range(2):
        for d in range(1, tms):

            @pl.when(tm + d < tms)
            def _():
                total_copy(stage, d).wait_send()


def writer(steps, heat, load, depth, harm, base, *refs):
    outs, total, sem = refs[:4], refs[4], refs[5]
    ins = (heat, load, depth, total)
    size = HALF

    def copy(i, k):
        part = pl.ds(k * size, size)
        return pltpu.make_async_copy(ins[i].at[part], outs[i].at[part], sem.at[i, k])

    for i in range(3):
        for k in range(PIECES):
            copy(i, k).start()
    for k in range(PIECES):
        part = pl.ds(k * size, size)
        total[part] = (harm[part] + base[k]) * (1.0 / steps)
        copy(3, k).start()
    for i in range(4):
        for k in range(PIECES):
            copy(i, k).wait()


def shards(tms, line, x, f, r, hh, hl, s0, p):
    modes, lags = r.shape
    steps = x.shape[1]
    points = hh.shape[1]
    nodes = RING * line * CORES
    every = nodes * modes
    hbm = pl.BlockSpec(memory_space=pltpu.HBM)
    vmem = pl.BlockSpec(memory_space=pltpu.VMEM)
    dma = pltpu.SemaphoreType.DMA
    sends = (line + 2) + 3 + 3 * (line - 2)
    arrays = (x, f, r, hh, hl, s0.reshape(1, points), p.reshape(1, points))
    results = pl.pallas_call(
        functools.partial(kernel, tms, line),
        out_shape=[pltpu.VMEM((steps, points), F32)] * 4 + [pltpu.VMEM((2, 1, points), F32)],
        in_specs=[hbm] * 7,
        out_specs=[vmem] * 5,
        scratch_shapes=[
            pltpu.VMEM((2 * modes, steps), BF16),
            pltpu.VMEM(f.shape, BF16),
            pltpu.VMEM((2 * modes, lags), F32),
            pltpu.VMEM((lags, 2 * modes), F32),
            pltpu.VMEM(hh.shape, BF16),
            pltpu.VMEM(hl.shape, BF16),
            pltpu.VMEM((1, points), F32),
            pltpu.VMEM((1, points), F32),
            pltpu.VMEM((modes, HALF), BF16),
            pltpu.VMEM((8, steps, 2 * modes), F32),
            pltpu.VMEM((8, HALF + 64, 2 * modes), F32),
            pltpu.VMEM((2, CORES, RING, line, modes, HALF), BF16),
            pltpu.VMEM((2, HALF, every), BF16),
            pltpu.VMEM((HALF, HALF), BF16),
            pltpu.VMEM((4, 1, points), F32),
            pltpu.VMEM((2, 1, points), F32),
            pltpu.VMEM((2, tms, 1, points), F32),
            dma((7 + 2 * RING * line,)),
            dma((line // 2 + 1,)),
            dma((2, sends)),
            dma((2, RING * line)),
            dma((2, 2, RING)),
            dma((2, tms)),
            dma((2, tms)),
            pltpu.SemaphoreType.REGULAR,
        ],
        compiler_params=pltpu.CompilerParams(
            collective_id=0, has_side_effects=True, vmem_limit_bytes=40 * 1024 * 1024
        ),
    )(*(pltpu.with_memory_space_constraint(a, pltpu.HBM) for a in arrays))
    return pl.pallas_call(
        functools.partial(writer, steps * tms),
        out_shape=[jax.ShapeDtypeStruct((steps, points), F32)] * 4,
        in_specs=[vmem] * 5,
        out_specs=[pl.BlockSpec(memory_space=pl.ANY)] * 4,
        scratch_shapes=[pltpu.VMEM((steps, points), F32), dma((4, PIECES))],
        compiler_params=pltpu.CompilerParams(vmem_limit_bytes=6 * 1024 * 1024),
    )(*results)


def solution(mesh):
    tms, nodes = mesh.shape["tm"], mesh.shape["node"]
    return jax.shard_map(
        functools.partial(shards, tms, nodes // (RING * CORES)),
        mesh=mesh,
        in_specs=(
            P(None, "tm"),
            P("node", None),
            P("node", None),
            P(None, "node"),
            P(None, "node"),
            P("node"),
            P("node"),
        ),
        out_specs=(P("tm", "node"),) * 4,
        check_vma=False,
    )
```

```python
import functools

import jax
import jax.numpy as jnp
from jax import lax
from jax.experimental import pallas as pl
from jax.experimental.pallas import tpu as pltpu
from jax.sharding import PartitionSpec as P

MESH = pl.DeviceIdType.MESH
F32, BF16 = jnp.float32, jnp.bfloat16
RING = 4
CORES = 2
HALF = 256
COLS = 256
PIECES = 2
NT = (((1,), (1,)), ((), ()))


def dot(a, b):
    return jnp.dot(a, b, preferred_element_type=F32)


def split_dot(tri, values):
    high = values.astype(BF16)
    low = (values - high.astype(F32)).astype(BF16)
    return dot(tri, high) + dot(tri, low)


def kernel(
    tms, line,
    x_in, f_in, r_in, hh_in, hl_in, s0_in, p_in,
    heat, load, depth, harm, base,
    x2, fv, rv, r2, hh, hl, s0, p, halo, ys, yh, g, lhs, tri, tot, mine, rec,
    in_sem, halo_sem, ssem, rsem, bsem, xs, xr, ready,
):
    tm = lax.axis_index("tm")
    me = lax.axis_index("node")
    core = lax.rem(me, CORES)
    z = lax.rem(me // CORES, line)
    x = me // (CORES * line)
    modes = f_in.shape[0]
    points = heat.shape[1]
    tiles = points // COLS

    def node(x, z, c):
        return (x * line + z) * CORES + c

    right, left, across = lax.rem(x + 1, RING), lax.rem(x + 3, RING), lax.rem(x + 2, RING)
    sib = node(x, z, 1 - core)
    others_x = (right, left, across)
    along_x = tuple(node(o, z, core) for o in others_x)
    if line == 4:
        upper = z // 2
        beside = 1 - z + 4 * upper
        others = (beside, lax.rem(z + 2, line), lax.rem(beside + 2, line))
    else:
        others = (1 - z,)
    along_z = tuple(node(x, o, core) for o in others)
    columns = (x, *others_x)
    chips = [a * line + b for a in columns for b in range(line)]
    both = CORES * modes

    barrier = pltpu.get_barrier_semaphore()

    span = tms // 2
    mid = line // 2
    crossed_in = 1 - lax.min(1, lax.rem(tm, span))
    crossed_out = 1 - lax.min(1, lax.rem(tm + 1, span))
    at_end = 1 - lax.min(1, lax.rem(z, line - 1))
    nearer = (line - 1) * (1 - z // mid)
    server = node(x, z + crossed_in * (nearer - z), core)
    served = (1 - (tm + 1) // tms) * (1 - crossed_out + crossed_out * at_end * mid)

    @pl.when(tm > 0)
    def _():
        pl.semaphore_signal(barrier, inc=1, device_id=(tm - 1, server), device_id_type=MESH)


    for d in range(1, tms):

        @pl.when(tm + d < tms)
        def _():
            pl.semaphore_signal(barrier, inc=1, device_id=(tm + d, me), device_id_type=MESH)

    for other in (sib, *along_x, *along_z):
        pl.semaphore_signal(barrier, inc=1, device_id=(tm, other), device_id_type=MESH)

    loads = [
        pltpu.make_async_copy(a, b, in_sem.at[i])
        for i, (a, b) in enumerate((
            (f_in, fv),
            (x_in, x2.at[pl.ds(modes, modes), :]),
            (x_in.at[:, pl.ds(0, HALF)], x2.at[pl.ds(0, modes), pl.ds(HALF, HALF)]),
            (r_in, rv.at[pl.ds(0, modes), :]),
            (r_in, rv.at[pl.ds(modes, modes), :]),
            (s0_in, s0),
            (p_in, p),
        ))
    ]

    def pattern_loads(i):
        there = pl.ds(pl.multiple_of(chips[i] * both, both), both)
        here = pl.ds(i * both, both)
        return [
            pltpu.make_async_copy(a.at[there], b.at[here], in_sem.at[7 + 2 * i + k])
            for k, (a, b) in enumerate(((hh_in, hh), (hl_in, hl)))
        ]

    for copy in loads:
        copy.start()
    for i in range(len(chips)):
        for copy in pattern_loads(i):
            copy.start()
    x2[pl.ds(0, modes), pl.ds(0, HALF)] = jnp.zeros((modes, HALF), BF16)
    tri[...] = (
        lax.broadcasted_iota(jnp.int32, (HALF, HALF), 0)
        >= lax.broadcasted_iota(jnp.int32, (HALF, HALF), 1)
    ).astype(F32).astype(BF16)
    for copy in loads[:5]:
        copy.wait()

    twice = (
        lax.rem(lax.broadcasted_iota(jnp.int32, (both, modes), 0), modes)
        == lax.broadcasted_iota(jnp.int32, (both, modes), 1)
    ).astype(F32).astype(BF16)
    wide = lax.dot_general(dot(twice, fv[...]).astype(BF16), twice, NT, preferred_element_type=F32)
    same = (
        lax.broadcasted_iota(jnp.int32, (both, both), 0) // modes
        == lax.broadcasted_iota(jnp.int32, (both, both), 1) // modes
    )
    drive = jnp.where(same, wide, 0.0).astype(BF16)

    def driven(source):
        return lax.dot_general(
            source.astype(F32).T.astype(BF16), drive, NT, preferred_element_type=F32
        )

    r2[...] = rv[...].T
    y = driven(x2[...])
    for s in range(8):
        ys[s] = y if s == 0 else pltpu.roll(y, s, 0)

    def lags(source, rows, down=0):
        def some(a, total):
            at = pl.multiple_of(HALF - 8 * a, 8)
            weights = r2[pl.ds(pl.multiple_of(8 * a, 8), 8), :]
            for s in range(8):
                total = total + weights[s : s + 1, :] * source[s, pl.ds(at + down, rows), :]
            return total

        return some

    groups = HALF // 8
    turns = groups // 2 + groups // 2 * lax.min(1, tm // span)
    blocks = range(0, HALF, both)
    local = [
        lax.fori_loop(0, turns, lags(ys, both, i), jnp.zeros((both, both), F32)) for i in blocks
    ]

    pl.semaphore_wait(barrier, 4 + len(others) + tm + served)

    def halo_copy(i):
        there = z + crossed_out * (i + mid * (1 - lax.min(1, z)) - z)
        return pltpu.make_async_remote_copy(
            src_ref=x2.at[pl.ds(modes, modes), pl.ds(HALF, HALF)],
            dst_ref=halo,
            send_sem=halo_sem.at[i],
            recv_sem=halo_sem.at[mid],
            device_id=(lax.rem(tm + 1, tms), node(x, there, core)),
            device_id_type=MESH,
        )

    def block(q, a, b, to, i):
        place = g.at[q, core, a, b]
        return pltpu.make_async_remote_copy(
            src_ref=place,
            dst_ref=place,
            send_sem=ssem.at[q, i],
            recv_sem=rsem.at[q, a * line + b],
            device_id=(tm, to),
            device_id_type=MESH,
        )

    def whole(q, a, c, i):
        place = g.at[q, c, a]
        return pltpu.make_async_remote_copy(
            src_ref=place,
            dst_ref=place,
            send_sem=bsem.at[0, q, i],
            recv_sem=bsem.at[1, q, a],
            device_id=(tm, sib),
            device_id_type=MESH,
        )

    def arrived(q, a, b):
        block(q, a, b, sib, 0).wait_recv()

    sent = [0, 0]

    def send(q, a, b, to):
        block(q, a, b, to, sent[q]).start()
        sent[q] += 1

    def own(q):
        for to in (*along_z[1:], *along_x[::-1], along_z[0]):
            send(q, x, z, to)

    def line_in(q, i):
        arrived(q, x, others[i])
        if i > 0:
            for to in along_x[::-1]:
                send(q, x, others[i], to)

    def ring_in(q, i):
        arrived(q, others_x[i], z)
        send(q, others_x[i], z, along_z[0])

    def near_in():
        for q in range(2):
            for i in range(1, len(others)):
                line_in(q, i)
            for i in range(3):
                ring_in(q, i)
        for q in range(2):
            line_in(q, 0)
            whole(q, x, core, 0).start()

    def far_in(q, i):
        for b in others:
            arrived(q, columns[i], b)
        whole(q, columns[i], core, i).start()

    def turn(q, i):
        whole(q, columns[i], 1 - core, i).wait_recv()
        for b in range(line):
            pair = g[q, :, columns[i], b].reshape(both, HALF)
            lhs[q, :, pl.ds((i * line + b) * both, both)] = pair.T

    def rows(q):
        return pl.ds(HALF * (1 - q), HALF)

    def tile(j):
        return pl.ds(j * COLS, COLS)

    width = line * both

    def add_columns(out, patterns, q, first, count, nodes=pl.ds(0, points)):
        some = pl.ds(first * width, count * width)
        value = dot(lhs[q, :, some], patterns[some, nodes])
        out[rows(q), nodes] = value if first == 0 else out[rows(q), nodes] + value

    per = tiles // 2
    ranges = [pl.ds(h * per * COLS, per * COLS) for h in range(2)]

    def in_range(h):
        return range(h * per, (h + 1) * per)

    def grow(q, h):
        for j in in_range(h):
            cols = tile(j)
            growth = p[:, cols] * jnp.exp(0.5 * heat[rows(q), cols])
            depth[rows(q), cols] = growth
            tot[q, :, cols] = jnp.sum(growth, axis=0, keepdims=True)

    def run_up(out, q):
        for j in range(tiles):
            cols = tile(j)
            out[rows(q), cols] = split_dot(tri[...], out[rows(q), cols])

    share = 8.0 / (2 * HALF * tms)

    def settle(q):
        run_up(depth, q)
        for j in range(tiles):
            cols = tile(j)
            start = s0[:, cols] * s0[:, cols]
            if q == 0:
                start = start + share * tot[1, :, cols]
            depth[rows(q), cols] = start + share * depth[rows(q), cols]

    for i in range(mid):

        @pl.when(served > i)
        def _():
            halo_copy(i).start()

    for d in range(1, tms):

        @pl.when(tm >= d)
        def _():
            pl.semaphore_signal(ready, inc=1, device_id=(tm - d, me), device_id_type=MESH)

    local = [
        lax.fori_loop(turns, groups, lags(ys, both, i), some) for i, some in zip(blocks, local)
    ]
    local = jnp.concatenate(local, axis=0).T
    part = local[:modes]
    g[0, core, x, z] = local[modes:].astype(BF16)
    own(0)

    @pl.when(tm > 0)
    def _():
        halo_copy(0).wait_recv()

    @pl.when(tm == 0)
    def _():
        halo[...] = jnp.zeros_like(halo)

    before = halo[...]
    shifted = jnp.concatenate([before[:, both:], jnp.zeros((modes, HALF - both), BF16)], axis=1)
    y = driven(jnp.concatenate([before, shifted], axis=0))
    y = jnp.concatenate([y, jnp.zeros((64, both), F32)], axis=0)
    for s in range(8):
        yh[s] = y if s == 0 else pltpu.roll(y, s, 0)
    first = lax.fori_loop(0, 8, lags(yh, 64), jnp.zeros((64, both), F32))
    first = jnp.concatenate([first, jnp.zeros((both - 64, both), F32)], axis=0)
    late = lax.fori_loop(8, groups, lags(yh, both), first).T
    late = jnp.concatenate([late[:modes], late[modes:]], axis=1)
    g[1, core, x, z] = (part + late).astype(BF16)

    own(1)
    near_in()
    turn(0, 0)
    for copy in loads[5:]:
        copy.wait()
    for i in range(len(chips)):
        for copy in pattern_loads(i):
            copy.wait()
    rest = RING - 1
    add_columns(heat, hh, 0, 0, 1)
    add_columns(load, hl, 0, 0, 1)
    turn(1, 0)
    add_columns(heat, hh, 1, 0, 1)
    for i in range(1, RING):
        far_in(0, i)
    add_columns(load, hl, 1, 0, 1)
    for i in range(1, RING):
        turn(0, i)
    add_columns(heat, hh, 0, 1, rest)
    grow(0, 0)
    grow(0, 1)
    for i in range(1, RING):
        far_in(1, i)
    add_columns(load, hl, 0, 1, rest)
    for i in range(1, RING):
        turn(1, i)

    def total_copy(stage, h, d):
        return pltpu.make_async_remote_copy(
            src_ref=mine.at[stage, :, ranges[h]],
            dst_ref=rec.at[stage, tm, :, ranges[h]],
            send_sem=xs.at[stage, h, d],
            recv_sem=xr.at[stage, h, tm],
            device_id=(lax.rem(tm + d, tms), me),
            device_id_type=MESH,
        )

    def give(stage, h):
        nodes = ranges[h]
        mine[stage, :, nodes] = tot[2 * stage, :, nodes] + tot[2 * stage + 1, :, nodes]
        for d in range(tms - 1, 0, -1):

            @pl.when(tm + d < tms)
            def _():
                total_copy(stage, h, d).start()

    def take(stage, h):
        def one(i, total):
            pltpu.make_async_remote_copy(
                src_ref=mine.at[stage, :, ranges[h]],
                dst_ref=rec.at[stage, i, :, ranges[h]],
                send_sem=xs.at[stage, h, 0],
                recv_sem=xr.at[stage, h, i],
                device_id=(lax.rem(tm + 1, tms), me),
                device_id_type=MESH,
            ).wait_recv()
            return total + rec[stage, i, :, ranges[h]]

        return lax.fori_loop(0, tm, one, jnp.zeros((1, per * COLS), F32))

    add_columns(heat, hh, 1, 1, rest, ranges[0])
    grow(1, 0)

    @pl.when(tm + 1 < tms)
    def _():
        pl.semaphore_wait(ready, tms - 1 - tm)

    give(0, 0)
    add_columns(heat, hh, 1, 1, rest, ranges[1])
    grow(1, 1)
    give(0, 1)
    add_columns(load, hl, 1, 1, rest)
    settle(1)
    settle(0)

    for i in range(mid):

        @pl.when(served > i)
        def _():
            halo_copy(i).wait_send()

    for q in range(2):
        for i in range(sent[q]):
            block(q, x, z, sib, i).wait_send()
        for i in range(RING):
            whole(q, x, core, i).wait_send()

    share = 8.0 / (2 * HALF * tms)

    def depth_tile(q, j):
        cols = tile(j)
        square = rec[0, tm, :, cols] + depth[rows(q), cols]
        layer = square * lax.rsqrt(square)
        depth[rows(q), cols] = layer
        stress = load[rows(q), cols] * (5.0 - 40.0 / (layer + 10.0))
        increment = stress * stress
        harm[rows(q), cols] = increment
        tot[2 + q, :, cols] = jnp.sum(increment, axis=0, keepdims=True)

    for h in range(2):
        rec[0, tm, :, ranges[h]] = share * take(0, h)
        for j in in_range(h):
            depth_tile(1, j)
            depth_tile(0, j)
        give(1, h)
    run_up(harm, 1)
    run_up(harm, 0)
    for h in range(2):
        earlier = take(1, h)
        base[0, :, ranges[h]] = earlier
        base[1, :, ranges[h]] = earlier + tot[3, :, ranges[h]]

    for stage in range(2):
        for h in range(2):
            for d in range(1, tms):

                @pl.when(tm + d < tms)
                def _():
                    total_copy(stage, h, d).wait_send()


def writer(steps, heat, load, depth, harm, base, *refs):
    outs, total, sem = refs[:4], refs[4], refs[5]
    ins = (heat, load, depth, total)
    size = HALF

    def copy(i, k):
        part = pl.ds(k * size, size)
        return pltpu.make_async_copy(ins[i].at[part], outs[i].at[part], sem.at[i, k])

    for i in range(3):
        for k in range(PIECES):
            copy(i, k).start()
    for k in range(PIECES):
        part = pl.ds(k * size, size)
        total[part] = (harm[part] + base[k]) * (1.0 / steps)
        copy(3, k).start()
    for i in range(4):
        for k in range(PIECES):
            copy(i, k).wait()


def shards(tms, line, x, f, r, hh, hl, s0, p):
    modes, lags = r.shape
    steps = x.shape[1]
    points = hh.shape[1]
    nodes = RING * line * CORES
    every = nodes * modes
    hbm = pl.BlockSpec(memory_space=pltpu.HBM)
    vmem = pl.BlockSpec(memory_space=pltpu.VMEM)
    dma = pltpu.SemaphoreType.DMA
    sends = (line + 2) + 3 + 3 * (line - 2)
    arrays = (x, f, r, hh, hl, s0.reshape(1, points), p.reshape(1, points))
    results = pl.pallas_call(
        functools.partial(kernel, tms, line),
        out_shape=[pltpu.VMEM((steps, points), F32)] * 4 + [pltpu.VMEM((2, 1, points), F32)],
        in_specs=[hbm] * 7,
        out_specs=[vmem] * 5,
        scratch_shapes=[
            pltpu.VMEM((2 * modes, steps), BF16),
            pltpu.VMEM(f.shape, BF16),
            pltpu.VMEM((2 * modes, lags), F32),
            pltpu.VMEM((lags, 2 * modes), F32),
            pltpu.VMEM(hh.shape, BF16),
            pltpu.VMEM(hl.shape, BF16),
            pltpu.VMEM((1, points), F32),
            pltpu.VMEM((1, points), F32),
            pltpu.VMEM((modes, HALF), BF16),
            pltpu.VMEM((8, steps, 2 * modes), F32),
            pltpu.VMEM((8, HALF + 64, 2 * modes), F32),
            pltpu.VMEM((2, CORES, RING, line, modes, HALF), BF16),
            pltpu.VMEM((2, HALF, every), BF16),
            pltpu.VMEM((HALF, HALF), BF16),
            pltpu.VMEM((4, 1, points), F32),
            pltpu.VMEM((2, 1, points), F32),
            pltpu.VMEM((2, tms, 1, points), F32),
            dma((7 + 2 * RING * line,)),
            dma((line // 2 + 1,)),
            dma((2, sends)),
            dma((2, RING * line)),
            dma((2, 2, RING)),
            dma((2, 2, tms)),
            dma((2, 2, tms)),
            pltpu.SemaphoreType.REGULAR,
        ],
        compiler_params=pltpu.CompilerParams(
            collective_id=0, has_side_effects=True, vmem_limit_bytes=40 * 1024 * 1024
        ),
    )(*(pltpu.with_memory_space_constraint(a, pltpu.HBM) for a in arrays))
    return pl.pallas_call(
        functools.partial(writer, steps * tms),
        out_shape=[jax.ShapeDtypeStruct((steps, points), F32)] * 4,
        in_specs=[vmem] * 5,
        out_specs=[pl.BlockSpec(memory_space=pl.ANY)] * 4,
        scratch_shapes=[pltpu.VMEM((steps, points), F32), dma((4, PIECES))],
        compiler_params=pltpu.CompilerParams(vmem_limit_bytes=6 * 1024 * 1024),
    )(*results)


def solution(mesh):
    tms, nodes = mesh.shape["tm"], mesh.shape["node"]
    return jax.shard_map(
        functools.partial(shards, tms, nodes // (RING * CORES)),
        mesh=mesh,
        in_specs=(
            P(None, "tm"),
            P("node", None),
            P("node", None),
            P(None, "node"),
            P(None, "node"),
            P("node"),
            P("node"),
        ),
        out_specs=(P("tm", "node"),) * 4,
        check_vma=False,
    )
```

```python
import functools

import jax
import jax.numpy as jnp
from jax import lax
from jax.experimental import pallas as pl
from jax.experimental.pallas import tpu as pltpu
from jax.sharding import PartitionSpec as P

MESH = pl.DeviceIdType.MESH
F32, BF16 = jnp.float32, jnp.bfloat16
RING = 4
CORES = 2
HALF = 256
COLS = 256
PIECES = 2
NT = (((1,), (1,)), ((), ()))


def dot(a, b):
    return jnp.dot(a, b, preferred_element_type=F32)


def split_dot(tri, values):
    high = values.astype(BF16)
    low = (values - high.astype(F32)).astype(BF16)
    return dot(tri, high) + dot(tri, low)


def kernel(
    tms, line,
    x_in, f_in, r_in, hh_in, hl_in, s0_in, p_in,
    heat, load, depth, harm, base,
    x2, fv, rv, r2, hh, hl, s0, p, halo, ys, yh, g, lhs, tri, tot, mine, rec,
    in_sem, halo_sem, ssem, rsem, bsem, xs, xr, ready,
):
    tm = lax.axis_index("tm")
    me = lax.axis_index("node")
    core = lax.rem(me, CORES)
    z = lax.rem(me // CORES, line)
    x = me // (CORES * line)
    modes = f_in.shape[0]
    points = heat.shape[1]
    tiles = points // COLS

    def node(x, z, c):
        return (x * line + z) * CORES + c

    right, left, across = lax.rem(x + 1, RING), lax.rem(x + 3, RING), lax.rem(x + 2, RING)
    sib = node(x, z, 1 - core)
    others_x = (right, left, across)
    along_x = tuple(node(o, z, core) for o in others_x)
    if line == 4:
        upper = z // 2
        beside = 1 - z + 4 * upper
        others = (beside, lax.rem(z + 2, line), lax.rem(beside + 2, line))
    else:
        others = (1 - z,)
    along_z = tuple(node(x, o, core) for o in others)
    columns = (x, *others_x)
    chips = [a * line + b for a in columns for b in range(line)]
    both = CORES * modes

    barrier = pltpu.get_barrier_semaphore()

    span = tms // 2
    mid = line // 2
    crossed_in = 1 - lax.min(1, lax.rem(tm, span))
    crossed_out = 1 - lax.min(1, lax.rem(tm + 1, span))
    at_end = 1 - lax.min(1, lax.rem(z, line - 1))
    nearer = (line - 1) * (1 - z // mid)
    server = node(x, z + crossed_in * (nearer - z), core)
    served = (1 - (tm + 1) // tms) * (1 - crossed_out + crossed_out * at_end * mid)

    @pl.when(tm > 0)
    def _():
        pl.semaphore_signal(barrier, inc=1, device_id=(tm - 1, server), device_id_type=MESH)


    for d in range(1, tms):

        @pl.when(tm + d < tms)
        def _():
            pl.semaphore_signal(barrier, inc=1, device_id=(tm + d, me), device_id_type=MESH)

    for other in (sib, *along_x, *along_z):
        pl.semaphore_signal(barrier, inc=1, device_id=(tm, other), device_id_type=MESH)

    loads = [
        pltpu.make_async_copy(a, b, in_sem.at[i])
        for i, (a, b) in enumerate((
            (f_in, fv),
            (x_in, x2.at[pl.ds(modes, modes), :]),
            (x_in.at[:, pl.ds(0, HALF)], x2.at[pl.ds(0, modes), pl.ds(HALF, HALF)]),
            (r_in, rv.at[pl.ds(0, modes), :]),
            (r_in, rv.at[pl.ds(modes, modes), :]),
            (s0_in, s0),
            (p_in, p),
        ))
    ]

    def pattern_loads(i):
        there = pl.ds(pl.multiple_of(chips[i] * both, both), both)
        here = pl.ds(i * both, both)
        return [
            pltpu.make_async_copy(a.at[there], b.at[here], in_sem.at[7 + 2 * i + k])
            for k, (a, b) in enumerate(((hh_in, hh), (hl_in, hl)))
        ]

    for copy in loads:
        copy.start()
    for i in range(len(chips)):
        for copy in pattern_loads(i):
            copy.start()
    x2[pl.ds(0, modes), pl.ds(0, HALF)] = jnp.zeros((modes, HALF), BF16)
    tri[...] = (
        lax.broadcasted_iota(jnp.int32, (HALF, HALF), 0)
        >= lax.broadcasted_iota(jnp.int32, (HALF, HALF), 1)
    ).astype(F32).astype(BF16)
    for copy in loads[:5]:
        copy.wait()

    force = fv[...].astype(F32)
    none = jnp.zeros_like(force)
    drive = jnp.concatenate(
        [jnp.concatenate([force, none], axis=1), jnp.concatenate([none, force], axis=1)], axis=0
    ).astype(BF16)

    def driven(source):
        return lax.dot_general(
            source.astype(F32).T.astype(BF16), drive, NT, preferred_element_type=F32
        )

    r2[...] = rv[...].T
    y = driven(x2[...])
    for s in range(8):
        ys[s] = y if s == 0 else pltpu.roll(y, s, 0)

    def lags(source, rows, down=0):
        def some(a, total):
            at = pl.multiple_of(HALF - 8 * a, 8)
            weights = r2[pl.ds(pl.multiple_of(8 * a, 8), 8), :]
            for s in range(8):
                total = total + weights[s : s + 1, :] * source[s, pl.ds(at + down, rows), :]
            return total

        return some

    groups = HALF // 8
    turns = groups // 2 + groups // 2 * lax.min(1, tm // span)
    blocks = range(0, HALF, both)
    local = [
        lax.fori_loop(0, turns, lags(ys, both, i), jnp.zeros((both, both), F32)) for i in blocks
    ]

    pl.semaphore_wait(barrier, 4 + len(others) + tm + served)

    def halo_copy(i):
        there = z + crossed_out * (i + mid * (1 - lax.min(1, z)) - z)
        return pltpu.make_async_remote_copy(
            src_ref=x2.at[pl.ds(modes, modes), pl.ds(HALF, HALF)],
            dst_ref=halo,
            send_sem=halo_sem.at[i],
            recv_sem=halo_sem.at[mid],
            device_id=(lax.rem(tm + 1, tms), node(x, there, core)),
            device_id_type=MESH,
        )

    def block(q, a, b, to, i):
        place = g.at[q, core, a, b]
        return pltpu.make_async_remote_copy(
            src_ref=place,
            dst_ref=place,
            send_sem=ssem.at[q, i],
            recv_sem=rsem.at[q, a * line + b],
            device_id=(tm, to),
            device_id_type=MESH,
        )

    def whole(q, a, c, i):
        place = g.at[q, c, a]
        return pltpu.make_async_remote_copy(
            src_ref=place,
            dst_ref=place,
            send_sem=bsem.at[0, q, i],
            recv_sem=bsem.at[1, q, a],
            device_id=(tm, sib),
            device_id_type=MESH,
        )

    def arrived(q, a, b):
        block(q, a, b, sib, 0).wait_recv()

    sent = [0, 0]

    def send(q, a, b, to):
        block(q, a, b, to, sent[q]).start()
        sent[q] += 1

    def own(q):
        for to in (*along_z[1:], *along_x[::-1], along_z[0]):
            send(q, x, z, to)

    def line_in(q, i):
        arrived(q, x, others[i])
        if i > 0:
            for to in along_x[::-1]:
                send(q, x, others[i], to)

    def ring_in(q, i):
        arrived(q, others_x[i], z)
        send(q, others_x[i], z, along_z[0])

    def near_in():
        for q in range(2):
            for i in range(1, len(others)):
                line_in(q, i)
            for i in range(3):
                ring_in(q, i)
        for q in range(2):
            line_in(q, 0)
            whole(q, x, core, 0).start()

    def far_in(q, i):
        for b in others:
            arrived(q, columns[i], b)
        whole(q, columns[i], core, i).start()

    def turn(q, i):
        whole(q, columns[i], 1 - core, i).wait_recv()
        for b in range(line):
            pair = g[q, :, columns[i], b].reshape(both, HALF)
            lhs[q, :, pl.ds((i * line + b) * both, both)] = pair.T

    def rows(q):
        return pl.ds(HALF * (1 - q), HALF)

    def tile(j):
        return pl.ds(j * COLS, COLS)

    width = line * both

    def add_columns(out, patterns, q, first, count, nodes=pl.ds(0, points)):
        some = pl.ds(first * width, count * width)
        value = dot(lhs[q, :, some], patterns[some, nodes])
        out[rows(q), nodes] = value if first == 0 else out[rows(q), nodes] + value

    per = tiles // 2
    ranges = [pl.ds(h * per * COLS, per * COLS) for h in range(2)]

    def in_range(h):
        return range(h * per, (h + 1) * per)

    def grow(q, h):
        for j in in_range(h):
            cols = tile(j)
            growth = p[:, cols] * jnp.exp(0.5 * heat[rows(q), cols])
            depth[rows(q), cols] = growth
            tot[q, :, cols] = jnp.sum(growth, axis=0, keepdims=True)

    def run_up(out, q):
        for j in range(tiles):
            cols = tile(j)
            out[rows(q), cols] = split_dot(tri[...], out[rows(q), cols])

    share = 8.0 / (2 * HALF * tms)

    def settle(q):
        run_up(depth, q)
        for j in range(tiles):
            cols = tile(j)
            start = s0[:, cols] * s0[:, cols]
            if q == 0:
                start = start + share * tot[1, :, cols]
            depth[rows(q), cols] = start + share * depth[rows(q), cols]

    for i in range(mid):

        @pl.when(served > i)
        def _():
            halo_copy(i).start()

    for d in range(1, tms):

        @pl.when(tm >= d)
        def _():
            pl.semaphore_signal(ready, inc=1, device_id=(tm - d, me), device_id_type=MESH)

    local = [
        lax.fori_loop(turns, groups, lags(ys, both, i), some) for i, some in zip(blocks, local)
    ]
    local = jnp.concatenate(local, axis=0).T
    part = local[:modes]
    g[0, core, x, z] = local[modes:].astype(BF16)
    own(0)

    @pl.when(tm > 0)
    def _():
        halo_copy(0).wait_recv()

    @pl.when(tm == 0)
    def _():
        halo[...] = jnp.zeros_like(halo)

    before = halo[...]
    shifted = jnp.concatenate([before[:, both:], jnp.zeros((modes, HALF - both), BF16)], axis=1)
    y = driven(jnp.concatenate([before, shifted], axis=0))
    y = jnp.concatenate([y, jnp.zeros((64, both), F32)], axis=0)
    for s in range(8):
        yh[s] = y if s == 0 else pltpu.roll(y, s, 0)
    first = lax.fori_loop(0, 8, lags(yh, 64), jnp.zeros((64, both), F32))
    first = jnp.concatenate([first, jnp.zeros((both - 64, both), F32)], axis=0)
    late = lax.fori_loop(8, groups, lags(yh, both), first).T
    late = jnp.concatenate([late[:modes], late[modes:]], axis=1)
    g[1, core, x, z] = (part + late).astype(BF16)

    own(1)
    near_in()
    turn(0, 0)
    for copy in loads[5:]:
        copy.wait()
    for i in range(len(chips)):
        for copy in pattern_loads(i):
            copy.wait()
    rest = RING - 1
    add_columns(heat, hh, 0, 0, 1)
    add_columns(load, hl, 0, 0, 1)
    turn(1, 0)
    add_columns(heat, hh, 1, 0, 1)
    for i in range(1, RING):
        far_in(0, i)
    add_columns(load, hl, 1, 0, 1)
    for i in range(1, RING):
        turn(0, i)
    add_columns(heat, hh, 0, 1, rest)
    grow(0, 0)
    grow(0, 1)
    for i in range(1, RING):
        far_in(1, i)
    add_columns(load, hl, 0, 1, rest)
    for i in range(1, RING):
        turn(1, i)

    def total_copy(stage, h, d):
        return pltpu.make_async_remote_copy(
            src_ref=mine.at[stage, :, ranges[h]],
            dst_ref=rec.at[stage, tm, :, ranges[h]],
            send_sem=xs.at[stage, h, d],
            recv_sem=xr.at[stage, h, tm],
            device_id=(lax.rem(tm + d, tms), me),
            device_id_type=MESH,
        )

    def give(stage, h):
        nodes = ranges[h]
        mine[stage, :, nodes] = tot[2 * stage, :, nodes] + tot[2 * stage + 1, :, nodes]
        for d in range(tms - 1, 0, -1):

            @pl.when(tm + d < tms)
            def _():
                total_copy(stage, h, d).start()

    def take(stage, h):
        def one(i, total):
            pltpu.make_async_remote_copy(
                src_ref=mine.at[stage, :, ranges[h]],
                dst_ref=rec.at[stage, i, :, ranges[h]],
                send_sem=xs.at[stage, h, 0],
                recv_sem=xr.at[stage, h, i],
                device_id=(lax.rem(tm + 1, tms), me),
                device_id_type=MESH,
            ).wait_recv()
            return total + rec[stage, i, :, ranges[h]]

        return lax.fori_loop(0, tm, one, jnp.zeros((1, per * COLS), F32))

    add_columns(heat, hh, 1, 1, rest, ranges[0])
    grow(1, 0)

    @pl.when(tm + 1 < tms)
    def _():
        pl.semaphore_wait(ready, tms - 1 - tm)

    give(0, 0)
    add_columns(heat, hh, 1, 1, rest, ranges[1])
    grow(1, 1)
    give(0, 1)
    add_columns(load, hl, 1, 1, rest)
    settle(1)
    settle(0)

    for i in range(mid):

        @pl.when(served > i)
        def _():
            halo_copy(i).wait_send()

    for q in range(2):
        for i in range(sent[q]):
            block(q, x, z, sib, i).wait_send()
        for i in range(RING):
            whole(q, x, core, i).wait_send()

    share = 8.0 / (2 * HALF * tms)

    def depth_tile(q, j):
        cols = tile(j)
        square = rec[0, tm, :, cols] + depth[rows(q), cols]
        layer = square * lax.rsqrt(square)
        depth[rows(q), cols] = layer
        stress = load[rows(q), cols] * (5.0 - 40.0 / (layer + 10.0))
        increment = stress * stress
        harm[rows(q), cols] = increment
        tot[2 + q, :, cols] = jnp.sum(increment, axis=0, keepdims=True)

    for h in range(2):
        rec[0, tm, :, ranges[h]] = share * take(0, h)
        for j in in_range(h):
            depth_tile(1, j)
            depth_tile(0, j)
        give(1, h)
    run_up(harm, 1)
    run_up(harm, 0)
    for h in range(2):
        earlier = take(1, h)
        base[0, :, ranges[h]] = earlier
        base[1, :, ranges[h]] = earlier + tot[3, :, ranges[h]]

    for stage in range(2):
        for h in range(2):
            for d in range(1, tms):

                @pl.when(tm + d < tms)
                def _():
                    total_copy(stage, h, d).wait_send()


def writer(steps, heat, load, depth, harm, base, *refs):
    outs, total, sem = refs[:4], refs[4], refs[5]
    ins = (heat, load, depth, total)
    size = HALF

    def copy(i, k):
        part = pl.ds(k * size, size)
        return pltpu.make_async_copy(ins[i].at[part], outs[i].at[part], sem.at[i, k])

    for i in range(3):
        for k in range(PIECES):
            copy(i, k).start()
    for k in range(PIECES):
        part = pl.ds(k * size, size)
        total[part] = (harm[part] + base[k]) * (1.0 / steps)
        copy(3, k).start()
    for i in range(4):
        for k in range(PIECES):
            copy(i, k).wait()


def shards(tms, line, x, f, r, hh, hl, s0, p):
    modes, lags = r.shape
    steps = x.shape[1]
    points = hh.shape[1]
    nodes = RING * line * CORES
    every = nodes * modes
    hbm = pl.BlockSpec(memory_space=pltpu.HBM)
    vmem = pl.BlockSpec(memory_space=pltpu.VMEM)
    dma = pltpu.SemaphoreType.DMA
    sends = (line + 2) + 3 + 3 * (line - 2)
    arrays = (x, f, r, hh, hl, s0.reshape(1, points), p.reshape(1, points))
    results = pl.pallas_call(
        functools.partial(kernel, tms, line),
        out_shape=[pltpu.VMEM((steps, points), F32)] * 4 + [pltpu.VMEM((2, 1, points), F32)],
        in_specs=[hbm] * 7,
        out_specs=[vmem] * 5,
        scratch_shapes=[
            pltpu.VMEM((2 * modes, steps), BF16),
            pltpu.VMEM(f.shape, BF16),
            pltpu.VMEM((2 * modes, lags), F32),
            pltpu.VMEM((lags, 2 * modes), F32),
            pltpu.VMEM(hh.shape, BF16),
            pltpu.VMEM(hl.shape, BF16),
            pltpu.VMEM((1, points), F32),
            pltpu.VMEM((1, points), F32),
            pltpu.VMEM((modes, HALF), BF16),
            pltpu.VMEM((8, steps, 2 * modes), F32),
            pltpu.VMEM((8, HALF + 64, 2 * modes), F32),
            pltpu.VMEM((2, CORES, RING, line, modes, HALF), BF16),
            pltpu.VMEM((2, HALF, every), BF16),
            pltpu.VMEM((HALF, HALF), BF16),
            pltpu.VMEM((4, 1, points), F32),
            pltpu.VMEM((2, 1, points), F32),
            pltpu.VMEM((2, tms, 1, points), F32),
            dma((7 + 2 * RING * line,)),
            dma((line // 2 + 1,)),
            dma((2, sends)),
            dma((2, RING * line)),
            dma((2, 2, RING)),
            dma((2, 2, tms)),
            dma((2, 2, tms)),
            pltpu.SemaphoreType.REGULAR,
        ],
        compiler_params=pltpu.CompilerParams(
            collective_id=0, has_side_effects=True, vmem_limit_bytes=40 * 1024 * 1024
        ),
    )(*(pltpu.with_memory_space_constraint(a, pltpu.HBM) for a in arrays))
    return pl.pallas_call(
        functools.partial(writer, steps * tms),
        out_shape=[jax.ShapeDtypeStruct((steps, points), F32)] * 4,
        in_specs=[vmem] * 5,
        out_specs=[pl.BlockSpec(memory_space=pl.ANY)] * 4,
        scratch_shapes=[pltpu.VMEM((steps, points), F32), dma((4, PIECES))],
        compiler_params=pltpu.CompilerParams(vmem_limit_bytes=6 * 1024 * 1024),
    )(*results)


def solution(mesh):
    tms, nodes = mesh.shape["tm"], mesh.shape["node"]
    return jax.shard_map(
        functools.partial(shards, tms, nodes // (RING * CORES)),
        mesh=mesh,
        in_specs=(
            P(None, "tm"),
            P("node", None),
            P("node", None),
            P(None, "node"),
            P(None, "node"),
            P("node"),
            P("node"),
        ),
        out_specs=(P("tm", "node"),) * 4,
        check_vma=False,
    )
```

```python
import functools

import jax
import jax.numpy as jnp
from jax import lax
from jax.experimental import pallas as pl
from jax.experimental.pallas import tpu as pltpu
from jax.sharding import PartitionSpec as P

MESH = pl.DeviceIdType.MESH
F32, BF16 = jnp.float32, jnp.bfloat16
RING = 4
CORES = 2
HALF = 256
COLS = 256
PIECES = 2
NT = (((1,), (1,)), ((), ()))


def dot(a, b):
    return jnp.dot(a, b, preferred_element_type=F32)


def split_dot(tri, values):
    high = values.astype(BF16)
    low = (values - high.astype(F32)).astype(BF16)
    return dot(tri, high) + dot(tri, low)


def kernel(
    tms, line,
    x_in, f_in, r_in, hh_in, hl_in, s0_in, p_in,
    heat, load, depth, harm, base,
    x2, fv, rv, r2, hh, hl, s0, p, halo, ys, yh, g, lhs, tri, tot, mine, rec,
    in_sem, halo_sem, ssem, rsem, bsem, xs, xr, ready,
):
    tm = lax.axis_index("tm")
    me = lax.axis_index("node")
    core = lax.rem(me, CORES)
    z = lax.rem(me // CORES, line)
    x = me // (CORES * line)
    modes = f_in.shape[0]
    points = heat.shape[1]
    tiles = points // COLS

    def node(x, z, c):
        return (x * line + z) * CORES + c

    right, left, across = lax.rem(x + 1, RING), lax.rem(x + 3, RING), lax.rem(x + 2, RING)
    sib = node(x, z, 1 - core)
    others_x = (right, left, across)
    along_x = tuple(node(o, z, core) for o in others_x)
    if line == 4:
        upper = z // 2
        beside = 1 - z + 4 * upper
        others = (beside, lax.rem(z + 2, line), lax.rem(beside + 2, line))
    else:
        others = (1 - z,)
    along_z = tuple(node(x, o, core) for o in others)
    columns = (x, *others_x)
    chips = [a * line + b for a in columns for b in range(line)]
    both = CORES * modes

    barrier = pltpu.get_barrier_semaphore()

    span = tms // 2
    mid = line // 2
    crossed_in = 1 - lax.min(1, lax.rem(tm, span))
    crossed_out = 1 - lax.min(1, lax.rem(tm + 1, span))
    at_end = 1 - lax.min(1, lax.rem(z, line - 1))
    nearer = (line - 1) * (1 - z // mid)
    server = node(x, z + crossed_in * (nearer - z), core)
    served = (1 - (tm + 1) // tms) * (1 - crossed_out + crossed_out * at_end * mid)

    @pl.when(tm > 0)
    def _():
        pl.semaphore_signal(barrier, inc=1, device_id=(tm - 1, server), device_id_type=MESH)


    for d in range(1, tms):

        @pl.when(tm + d < tms)
        def _():
            pl.semaphore_signal(barrier, inc=1, device_id=(tm + d, me), device_id_type=MESH)

    for other in (sib, *along_x, *along_z):
        pl.semaphore_signal(barrier, inc=1, device_id=(tm, other), device_id_type=MESH)

    loads = [
        pltpu.make_async_copy(a, b, in_sem.at[i])
        for i, (a, b) in enumerate((
            (f_in, fv),
            (x_in, x2.at[pl.ds(modes, modes), :]),
            (x_in.at[:, pl.ds(0, HALF)], x2.at[pl.ds(0, modes), pl.ds(HALF, HALF)]),
            (r_in, rv.at[pl.ds(0, modes), :]),
            (r_in, rv.at[pl.ds(modes, modes), :]),
            (s0_in, s0),
            (p_in, p),
        ))
    ]

    def pattern_loads(i):
        there = pl.ds(pl.multiple_of(chips[i] * both, both), both)
        here = pl.ds(i * both, both)
        return [
            pltpu.make_async_copy(a.at[there], b.at[here], in_sem.at[7 + 2 * i + k])
            for k, (a, b) in enumerate(((hh_in, hh), (hl_in, hl)))
        ]

    for copy in loads:
        copy.start()
    for i in range(len(chips)):
        for copy in pattern_loads(i):
            copy.start()
    x2[pl.ds(0, modes), pl.ds(0, HALF)] = jnp.zeros((modes, HALF), BF16)
    tri[...] = (
        lax.broadcasted_iota(jnp.int32, (HALF, HALF), 0)
        >= lax.broadcasted_iota(jnp.int32, (HALF, HALF), 1)
    ).astype(F32).astype(BF16)
    loads[0].wait()

    force = fv[...].astype(F32)
    none = jnp.zeros_like(force)
    drive = jnp.concatenate(
        [jnp.concatenate([force, none], axis=1), jnp.concatenate([none, force], axis=1)], axis=0
    ).astype(BF16)

    def driven(source):
        return lax.dot_general(
            source.astype(F32).T.astype(BF16), drive, NT, preferred_element_type=F32
        )

    for copy in loads[1:3]:
        copy.wait()
    y = driven(x2[...])
    for s in range(8):
        ys[s] = y if s == 0 else pltpu.roll(y, s, 0)
    for copy in loads[3:5]:
        copy.wait()
    r2[...] = rv[...].T

    def lags(source, rows, down=0):
        def some(a, total):
            at = pl.multiple_of(HALF - 8 * a, 8)
            weights = r2[pl.ds(pl.multiple_of(8 * a, 8), 8), :]
            for s in range(8):
                total = total + weights[s : s + 1, :] * source[s, pl.ds(at + down, rows), :]
            return total

        return some

    groups = HALF // 8
    turns = groups // 2 + groups // 2 * lax.min(1, tm // span)
    blocks = range(0, HALF, both)
    local = [
        lax.fori_loop(0, turns, lags(ys, both, i), jnp.zeros((both, both), F32)) for i in blocks
    ]

    pl.semaphore_wait(barrier, 4 + len(others) + tm + served)

    def halo_copy(i):
        there = z + crossed_out * (i + mid * (1 - lax.min(1, z)) - z)
        return pltpu.make_async_remote_copy(
            src_ref=x2.at[pl.ds(modes, modes), pl.ds(HALF, HALF)],
            dst_ref=halo,
            send_sem=halo_sem.at[i],
            recv_sem=halo_sem.at[mid],
            device_id=(lax.rem(tm + 1, tms), node(x, there, core)),
            device_id_type=MESH,
        )

    def block(q, a, b, to, i):
        place = g.at[q, core, a, b]
        return pltpu.make_async_remote_copy(
            src_ref=place,
            dst_ref=place,
            send_sem=ssem.at[q, i],
            recv_sem=rsem.at[q, a * line + b],
            device_id=(tm, to),
            device_id_type=MESH,
        )

    def whole(q, a, c, i):
        place = g.at[q, c, a]
        return pltpu.make_async_remote_copy(
            src_ref=place,
            dst_ref=place,
            send_sem=bsem.at[0, q, i],
            recv_sem=bsem.at[1, q, a],
            device_id=(tm, sib),
            device_id_type=MESH,
        )

    def arrived(q, a, b):
        block(q, a, b, sib, 0).wait_recv()

    sent = [0, 0]

    def send(q, a, b, to):
        block(q, a, b, to, sent[q]).start()
        sent[q] += 1

    def own(q):
        for to in (*along_z[1:], *along_x[::-1], along_z[0]):
            send(q, x, z, to)

    def line_in(q, i):
        arrived(q, x, others[i])
        if i > 0:
            for to in along_x[::-1]:
                send(q, x, others[i], to)

    def ring_in(q, i):
        arrived(q, others_x[i], z)
        send(q, others_x[i], z, along_z[0])

    def near_in():
        for q in range(2):
            for i in range(1, len(others)):
                line_in(q, i)
            for i in range(3):
                ring_in(q, i)
        for q in range(2):
            line_in(q, 0)
            whole(q, x, core, 0).start()

    def far_in(q, i):
        for b in others:
            arrived(q, columns[i], b)
        whole(q, columns[i], core, i).start()

    def turn(q, i):
        whole(q, columns[i], 1 - core, i).wait_recv()
        for b in range(line):
            pair = g[q, :, columns[i], b].reshape(both, HALF)
            lhs[q, :, pl.ds((i * line + b) * both, both)] = pair.T

    def rows(q):
        return pl.ds(HALF * (1 - q), HALF)

    def tile(j):
        return pl.ds(j * COLS, COLS)

    width = line * both

    def add_columns(out, patterns, q, first, count, nodes=pl.ds(0, points)):
        some = pl.ds(first * width, count * width)
        value = dot(lhs[q, :, some], patterns[some, nodes])
        out[rows(q), nodes] = value if first == 0 else out[rows(q), nodes] + value

    per = tiles // 2
    ranges = [pl.ds(h * per * COLS, per * COLS) for h in range(2)]

    def in_range(h):
        return range(h * per, (h + 1) * per)

    def grow(q, h):
        for j in in_range(h):
            cols = tile(j)
            growth = p[:, cols] * jnp.exp(0.5 * heat[rows(q), cols])
            depth[rows(q), cols] = growth
            tot[q, :, cols] = jnp.sum(growth, axis=0, keepdims=True)

    def run_up(out, q):
        for j in range(tiles):
            cols = tile(j)
            out[rows(q), cols] = split_dot(tri[...], out[rows(q), cols])

    share = 8.0 / (2 * HALF * tms)

    def settle(q):
        run_up(depth, q)
        for j in range(tiles):
            cols = tile(j)
            start = s0[:, cols] * s0[:, cols]
            if q == 0:
                start = start + share * tot[1, :, cols]
            depth[rows(q), cols] = start + share * depth[rows(q), cols]

    for i in range(mid):

        @pl.when(served > i)
        def _():
            halo_copy(i).start()

    for d in range(1, tms):

        @pl.when(tm >= d)
        def _():
            pl.semaphore_signal(ready, inc=1, device_id=(tm - d, me), device_id_type=MESH)

    local = [
        lax.fori_loop(turns, groups, lags(ys, both, i), some) for i, some in zip(blocks, local)
    ]
    local = jnp.concatenate(local, axis=0).T
    part = local[:modes]
    g[0, core, x, z] = local[modes:].astype(BF16)
    own(0)

    @pl.when(tm > 0)
    def _():
        halo_copy(0).wait_recv()

    @pl.when(tm == 0)
    def _():
        halo[...] = jnp.zeros_like(halo)

    before = halo[...]
    shifted = jnp.concatenate([before[:, both:], jnp.zeros((modes, HALF - both), BF16)], axis=1)
    y = driven(jnp.concatenate([before, shifted], axis=0))
    y = jnp.concatenate([y, jnp.zeros((64, both), F32)], axis=0)
    for s in range(8):
        yh[s] = y if s == 0 else pltpu.roll(y, s, 0)
    first = lax.fori_loop(0, 8, lags(yh, 64), jnp.zeros((64, both), F32))
    first = jnp.concatenate([first, jnp.zeros((both - 64, both), F32)], axis=0)
    late = lax.fori_loop(8, groups, lags(yh, both), first).T
    late = jnp.concatenate([late[:modes], late[modes:]], axis=1)
    g[1, core, x, z] = (part + late).astype(BF16)

    own(1)
    near_in()
    turn(0, 0)
    for copy in loads[5:]:
        copy.wait()
    for i in range(len(chips)):
        for copy in pattern_loads(i):
            copy.wait()
    rest = RING - 1
    add_columns(heat, hh, 0, 0, 1)
    add_columns(load, hl, 0, 0, 1)
    turn(1, 0)
    add_columns(heat, hh, 1, 0, 1)
    for i in range(1, RING):
        far_in(0, i)
    add_columns(load, hl, 1, 0, 1)
    for i in range(1, RING):
        turn(0, i)
    add_columns(heat, hh, 0, 1, rest)
    grow(0, 0)
    grow(0, 1)
    for i in range(1, RING):
        far_in(1, i)
    add_columns(load, hl, 0, 1, rest)
    for i in range(1, RING):
        turn(1, i)

    def total_copy(stage, h, d):
        return pltpu.make_async_remote_copy(
            src_ref=mine.at[stage, :, ranges[h]],
            dst_ref=rec.at[stage, tm, :, ranges[h]],
            send_sem=xs.at[stage, h, d],
            recv_sem=xr.at[stage, h, tm],
            device_id=(lax.rem(tm + d, tms), me),
            device_id_type=MESH,
        )

    def give(stage, h):
        nodes = ranges[h]
        mine[stage, :, nodes] = tot[2 * stage, :, nodes] + tot[2 * stage + 1, :, nodes]
        for d in range(tms - 1, 0, -1):

            @pl.when(tm + d < tms)
            def _():
                total_copy(stage, h, d).start()

    def take(stage, h):
        def one(i, total):
            pltpu.make_async_remote_copy(
                src_ref=mine.at[stage, :, ranges[h]],
                dst_ref=rec.at[stage, i, :, ranges[h]],
                send_sem=xs.at[stage, h, 0],
                recv_sem=xr.at[stage, h, i],
                device_id=(lax.rem(tm + 1, tms), me),
                device_id_type=MESH,
            ).wait_recv()
            return total + rec[stage, i, :, ranges[h]]

        return lax.fori_loop(0, tm, one, jnp.zeros((1, per * COLS), F32))

    add_columns(heat, hh, 1, 1, rest, ranges[0])
    grow(1, 0)

    @pl.when(tm + 1 < tms)
    def _():
        pl.semaphore_wait(ready, tms - 1 - tm)

    give(0, 0)
    add_columns(heat, hh, 1, 1, rest, ranges[1])
    grow(1, 1)
    give(0, 1)
    add_columns(load, hl, 1, 1, rest)
    settle(1)
    settle(0)

    for i in range(mid):

        @pl.when(served > i)
        def _():
            halo_copy(i).wait_send()

    for q in range(2):
        for i in range(sent[q]):
            block(q, x, z, sib, i).wait_send()
        for i in range(RING):
            whole(q, x, core, i).wait_send()

    share = 8.0 / (2 * HALF * tms)

    def depth_tile(q, j):
        cols = tile(j)
        square = rec[0, tm, :, cols] + depth[rows(q), cols]
        layer = square * lax.rsqrt(square)
        depth[rows(q), cols] = layer
        stress = load[rows(q), cols] * (5.0 - 40.0 / (layer + 10.0))
        increment = stress * stress
        harm[rows(q), cols] = increment
        tot[2 + q, :, cols] = jnp.sum(increment, axis=0, keepdims=True)

    for h in range(2):
        rec[0, tm, :, ranges[h]] = share * take(0, h)
        for j in in_range(h):
            depth_tile(1, j)
            depth_tile(0, j)
        give(1, h)
    run_up(harm, 1)
    run_up(harm, 0)
    for h in range(2):
        earlier = take(1, h)
        base[0, :, ranges[h]] = earlier
        base[1, :, ranges[h]] = earlier + tot[3, :, ranges[h]]

    for stage in range(2):
        for h in range(2):
            for d in range(1, tms):

                @pl.when(tm + d < tms)
                def _():
                    total_copy(stage, h, d).wait_send()


def writer(steps, heat, load, depth, harm, base, *refs):
    outs, total, sem = refs[:4], refs[4], refs[5]
    ins = (heat, load, depth, total)
    size = HALF

    def copy(i, k):
        part = pl.ds(k * size, size)
        return pltpu.make_async_copy(ins[i].at[part], outs[i].at[part], sem.at[i, k])

    for i in range(3):
        for k in range(PIECES):
            copy(i, k).start()
    for k in range(PIECES):
        part = pl.ds(k * size, size)
        total[part] = (harm[part] + base[k]) * (1.0 / steps)
        copy(3, k).start()
    for i in range(4):
        for k in range(PIECES):
            copy(i, k).wait()


def shards(tms, line, x, f, r, hh, hl, s0, p):
    modes, lags = r.shape
    steps = x.shape[1]
    points = hh.shape[1]
    nodes = RING * line * CORES
    every = nodes * modes
    hbm = pl.BlockSpec(memory_space=pltpu.HBM)
    vmem = pl.BlockSpec(memory_space=pltpu.VMEM)
    dma = pltpu.SemaphoreType.DMA
    sends = (line + 2) + 3 + 3 * (line - 2)
    arrays = (x, f, r, hh, hl, s0.reshape(1, points), p.reshape(1, points))
    results = pl.pallas_call(
        functools.partial(kernel, tms, line),
        out_shape=[pltpu.VMEM((steps, points), F32)] * 4 + [pltpu.VMEM((2, 1, points), F32)],
        in_specs=[hbm] * 7,
        out_specs=[vmem] * 5,
        scratch_shapes=[
            pltpu.VMEM((2 * modes, steps), BF16),
            pltpu.VMEM(f.shape, BF16),
            pltpu.VMEM((2 * modes, lags), F32),
            pltpu.VMEM((lags, 2 * modes), F32),
            pltpu.VMEM(hh.shape, BF16),
            pltpu.VMEM(hl.shape, BF16),
            pltpu.VMEM((1, points), F32),
            pltpu.VMEM((1, points), F32),
            pltpu.VMEM((modes, HALF), BF16),
            pltpu.VMEM((8, steps, 2 * modes), F32),
            pltpu.VMEM((8, HALF + 64, 2 * modes), F32),
            pltpu.VMEM((2, CORES, RING, line, modes, HALF), BF16),
            pltpu.VMEM((2, HALF, every), BF16),
            pltpu.VMEM((HALF, HALF), BF16),
            pltpu.VMEM((4, 1, points), F32),
            pltpu.VMEM((2, 1, points), F32),
            pltpu.VMEM((2, tms, 1, points), F32),
            dma((7 + 2 * RING * line,)),
            dma((line // 2 + 1,)),
            dma((2, sends)),
            dma((2, RING * line)),
            dma((2, 2, RING)),
            dma((2, 2, tms)),
            dma((2, 2, tms)),
            pltpu.SemaphoreType.REGULAR,
        ],
        compiler_params=pltpu.CompilerParams(
            collective_id=0, has_side_effects=True, vmem_limit_bytes=40 * 1024 * 1024
        ),
    )(*(pltpu.with_memory_space_constraint(a, pltpu.HBM) for a in arrays))
    return pl.pallas_call(
        functools.partial(writer, steps * tms),
        out_shape=[jax.ShapeDtypeStruct((steps, points), F32)] * 4,
        in_specs=[vmem] * 5,
        out_specs=[pl.BlockSpec(memory_space=pl.ANY)] * 4,
        scratch_shapes=[pltpu.VMEM((steps, points), F32), dma((4, PIECES))],
        compiler_params=pltpu.CompilerParams(vmem_limit_bytes=6 * 1024 * 1024),
    )(*results)


def solution(mesh):
    tms, nodes = mesh.shape["tm"], mesh.shape["node"]
    return jax.shard_map(
        functools.partial(shards, tms, nodes // (RING * CORES)),
        mesh=mesh,
        in_specs=(
            P(None, "tm"),
            P("node", None),
            P("node", None),
            P(None, "node"),
            P(None, "node"),
            P("node"),
            P("node"),
        ),
        out_specs=(P("tm", "node"),) * 4,
        check_vma=False,
    )
```
